512 devices in a mesh: leaf: 32 (over x_hi, z), grid: 16 (over x_lo, y, core).
Axes of the slice: x: 4 (x_hi: 2, x_lo: 2; x = x_hi * 2 + x_lo), y: 4, z: 16, core: 2. Of those that a mesh axis runs over, the one named last changes fastest.
Arguments:
- ancestor_inverse: bfloat16 [2048, 2048], P('grid', 'leaf')
- factor_block: bfloat16 [32, 2048, 4096], P('leaf', 'grid'), may hold values from -0.25 to 0.25
- block_pattern: int32 [32, 16], P('leaf'), may hold values 0 or 1
- pivot_inverse: float32 [32, 4096], P('leaf', 'grid'), may hold values from 0.5 to 2
Outputs:
- cross_cov: bfloat16 [32, 2048, 4096], P('leaf', 'grid')
- variances: float32 [32, 4096], P('leaf', 'grid')
The draws below stay inside these ranges and needn't reach their ends.
All inputs are finite; a program needn't handle non-finite values. No bound on the sum of `block_pattern` on one device may be relied on, other than what follows from the above.
Results may differ from the reference program's by a relative error of at most 0.0004.
Values may be sent and summed in bfloat16 or wider, within the bound.
A program may use at most 64 MiB of HBM per device.

```python
import math
import jax
import jax.numpy as jnp
from jax import lax

WR = 2048
WJ = 4096
NBLK = 16
CHILDREN = 32


def draw_ancestor_inverse(key, part):
    key = jax.random.fold_in(key, 7)
    key_diag, key_off = jax.random.split(key)
    scales = jnp.exp(jax.random.uniform(key_diag, (WR,), jnp.float32, jnp.log(0.5), jnp.log(2.0)))
    noise = jax.random.normal(key_off, (WR, WR), jnp.float32)
    spread = 0.2 / jnp.sqrt(2.0 * WR)
    offdiag = (noise + noise.T) * spread
    return (jnp.diag(scales) + offdiag).astype(jnp.bfloat16)


def plant(result, key, least, top_value):
    spot = [jax.random.randint(jax.random.fold_in(key, axis), (), 0, length) for axis, length in enumerate(result.shape)]
    main_axis = result.shape.index(max(result.shape))
    beside = spot[:main_axis] + [(spot[main_axis] + 1) % result.shape[main_axis]] + spot[main_axis + 1:]
    return result.at[tuple(spot)].set(least).at[tuple(beside)].set(top_value)


def level_of(own_key, extent, shards, least, largest):
    def one(dim, parts):
        steps = jax.random.uniform(jax.random.fold_in(jax.random.fold_in(own_key, 6), dim), (parts,), jnp.float32, least / len(shards), largest / len(shards))
        return jnp.repeat(jnp.exp(steps), extent[dim] // parts).reshape((-1,) + (1,) * (len(extent) - dim - 1))

    factor_of = one(*shards[0])
    for cut in shards[1:]:
        factor_of = factor_of * one(*cut)
    return factor_of


def normal_values(key, shape, deviation, reach, cuts=(), kind=jnp.bfloat16):
    entries = jax.random.normal(key, shape, jnp.float32) * deviation
    if len(cuts) > 0:
        entries = level_of(key, shape, cuts, -0.22, 0.18) * entries
    return jnp.clip(entries, min=-reach, max=reach).astype(kind)


def setup_inputs(seed: int = 0) -> dict:
    arg_keys = jax.random.split(jax.random.key(seed), 5)
    ancestor_inverse = draw_ancestor_inverse(jax.random.fold_in(arg_keys[4], 71), 0)
    factor_block = normal_values(arg_keys[1], (CHILDREN, WR, WJ), (WR // 4) ** -0.5, 0.25, ((0, 32), (1, 16)))
    block_pattern = plant((jax.random.randint(arg_keys[2], (CHILDREN, NBLK), 0, 4) < 3).astype(jnp.int32), jax.random.fold_in(arg_keys[2], 1), 0, 1)
    pivot_inverse = jnp.clip(jnp.exp(math.log(2.0) - 1.3862944 * jax.random.uniform(arg_keys[3], (CHILDREN, WJ), jnp.float32) ** level_of(arg_keys[3], (CHILDREN, WJ), ((0, 32), (1, 16)), -0.2, 0.2)), 0.5, 2.0)
    return dict(ancestor_inverse=ancestor_inverse, factor_block=factor_block, block_pattern=block_pattern, pivot_inverse=pivot_inverse)


def reference(ancestor_inverse, factor_block, block_pattern, pivot_inverse):
    rows_per = WR // NBLK
    row_ids = jnp.arange(WR, dtype=jnp.int32) // rows_per

    def one_child(items):
        factor, pattern, pivots = items
        keep = jnp.take(pattern, row_ids).astype(jnp.bfloat16)
        masked = factor * keep[:, None]
        cross = -jnp.dot(ancestor_inverse, masked, preferred_element_type=jnp.float32)
        variance = pivots - jnp.sum(masked.astype(jnp.float32) * cross, axis=0)
        return cross.astype(jnp.bfloat16), variance

    cross_cov, variances = lax.map(one_child, (factor_block, block_pattern, pivot_inverse))
    return cross_cov, variances
```

```python
import jax
import jax.numpy as jnp
from jax import lax
from jax.experimental import pallas as pl
from jax.experimental.pallas import tpu as pltpu
from jax.sharding import PartitionSpec as P

MESH = pl.DeviceIdType.MESH
F32, BF16 = jnp.float32, jnp.bfloat16
NX, NY, NC, NZ = 2, 4, 2, 16
ROWS, SEG = 128, 256
AHEAD = 1
PASSES = (2, 1, 3, 0)


def kernel(
    a_ref, f_ref, pat_ref, piv_ref, out_ref, var_ref,
    raw, masked, anc, place, got, cov, vpart, vgot,
    m_send, x_send, m_recv, m_local, h_sem, t_send, t_recv,
    z_send, z_recv, c_send, c_recv, o_send, o_recv, o_local, v_sem,
):
    leaf, grid = lax.axis_index("leaf"), lax.axis_index("grid")
    xh, z = leaf // NZ, lax.rem(leaf, NZ)
    x, y, c = grid // (NY * NC), lax.rem(grid // NC, NY), lax.rem(grid, NC)

    def around_y(dy):
        return lax.rem(y + dy, NY)

    def around_z(dz):
        return lax.rem(z + dz + NZ, NZ)

    def core(dc):
        return lax.rem(c + dc, NC)

    def here(dy, dc):
        return (leaf, x * NY * NC + around_y(dy) * NC + core(dc))

    x_mate = (leaf, (1 - x) * NY * NC + y * NC + c)
    h_mate = ((1 - xh) * NZ + z, grid)
    z_next = (xh * NZ + around_z(1), grid)
    z_prev = (xh * NZ + around_z(-1), grid)

    def block(dy, dc):
        return around_y(dy) * NC + core(dc)

    def columns(s, b):
        return pl.ds(pl.multiple_of(s * NY * NC * SEG + b * SEG, SEG), SEG)

    others = [(dy, dc) for dy in (2, 1, 3) for dc in range(NC)] + [(0, 1)]
    sends = []

    def remote(src, dst, send, recv, to):
        return pltpu.make_async_remote_copy(
            src_ref=src, dst_ref=dst, send_sem=send, recv_sem=recv, device_id=to, device_id_type=MESH
        )

    def send(*copy):
        handle = remote(*copy)
        handle.start()
        sends.append(handle)

    barrier = pltpu.get_barrier_semaphore()
    known = [here(dy, dc) for dy, dc in others] + [x_mate, h_mate, z_next, z_prev]
    for to in known:
        pl.semaphore_signal(barrier, inc=1, device_id=to, device_id_type=MESH)
    own = a_ref[...]
    nil = jnp.zeros_like(own)
    place[...] = jnp.where(xh == 0, jnp.concatenate([own, nil], 1), jnp.concatenate([nil, own], 1))
    pl.semaphore_wait(barrier, len(known))

    h_copy = remote(place, got, h_sem.at[0], h_sem.at[1], h_mate)
    h_copy.start()

    me = block(0, 0)

    def slot(s, b, side):
        return raw.at[s, b, :, side]

    def scatter(s):
        mine = f_ref.at[:, :, columns(s, me)]
        send(mine, slot(s, me, x), x_send.at[s, 0], m_recv.at[s, x, me], x_mate)
        for k, (dy, dc) in enumerate(others):
            part = f_ref.at[:, :, columns(s, block(dy, dc))]
            send(part, slot(s, me, x), m_send.at[s, k], m_recv.at[s, x, me], here(dy, dc))
        local = pltpu.make_async_copy(mine, slot(s, me, x), m_local.at[s])
        local.start()
        return local

    def arrived(s, b, side):
        remote(slot(s, b, side), slot(s, b, side), x_send.at[s, 0], m_recv.at[s, side, b], x_mate).wait_recv()

    def pass_over(s, k):
        b = block(*others[k])
        arrived(s, b, x)
        send(slot(s, b, x), slot(s, b, x), x_send.at[s, k + 1], m_recv.at[s, x, b], x_mate)

    locals_ = [scatter(0)]

    h_copy.wait()
    anc[z, y, c] = place[...] + got[...]

    def ring(step, p, way, to):
        q = around_y(PASSES[p])
        part = anc.at[around_z(-step if way == 0 else step), q, c]
        send(part, part, z_send.at[way, step, p], z_recv.at[way, step, p], to)

    def to_core(origin, p):
        part = anc.at[around_z(-origin), around_y(PASSES[p]), c]
        send(part, part, c_send.at[origin % NZ, p], c_recv.at[origin % NZ, p], here(0, 1))

    def ring_both(p):
        ring(0, p, 0, z_next)
        ring(0, p, 1, z_prev)
        to_core(0, p)

    mine = anc.at[z, y, c]
    for k, dy in enumerate((2, 1, 3)):
        send(mine, mine, t_send.at[k], t_recv.at[dy], here(dy, 0))
    ring_both(PASSES.index(0))
    locals_.append(scatter(1))
    for dy in (1, 3, 2):
        part = anc.at[z, around_y(dy), c]
        remote(part, part, t_send.at[0], t_recv.at[NY - dy], here(dy, 0)).wait_recv()
        ring_both(PASSES.index(dy))

    for k in (6, 2, 3, 4, 5, 0, 1):
        pass_over(0, k)

    def ring_step(step, p):
        q = around_y(PASSES[p])
        for way, to in ((0, z_next), (1, z_prev)):
            if step == NZ // 2 and way != p % 2:
                continue
            origin = step if way == 0 else -step
            part = anc.at[around_z(-origin), q, c]
            remote(part, part, z_send.at[way, 0, p], z_recv.at[way, step - 1, p], to).wait_recv()
            if step < NZ // 2 - 1 or (step == NZ // 2 - 1 and way == p % 2):
                ring(step, p, way, to)
            to_core(origin, p)

    def mask(s):
        locals_[s].wait()
        for b in range(NY * NC):
            for side in range(NX):
                keep = jnp.full((2, 64, SEG), pat_ref[0, side * NY * NC + b].astype(F32), F32).astype(BF16)
                masked[s, b, :, side] = raw[s, b, :, side] * keep

    def gathered(s):
        for dy in range(NY):
            for dc in range(NC):
                arrived(s, block(dy, dc), 1 - x)
        mask(s)

    def pass_done(p):
        for origin in range(NZ):
            part = anc.at[around_z(-origin), around_y(PASSES[p]), core(1)]
            remote(part, part, c_send.at[0, p], c_recv.at[origin, p], here(0, 1)).wait_recv()

    def product(s, p):
        q = around_y(PASSES[p])
        total = jnp.zeros((NC * ROWS, SEG), F32)
        for k in range(NZ // 2):
            left = jnp.concatenate(
                [anc[2 * k, q].reshape(NC * ROWS, 128), anc[2 * k + 1, q].reshape(NC * ROWS, 128)], 1
            )
            total += jnp.dot(left, masked[s, k].reshape(256, SEG), preferred_element_type=F32)
        cross = -total
        rows = jnp.concatenate([masked[s, NC * q + cc, :, x].reshape(ROWS, SEG) for cc in range(NC)], 0)
        terms = rows.astype(F32) * cross
        vpart[s] += jnp.sum(terms.reshape(NC * ROWS // 8, 8, SEG), axis=0)
        cov[s, p] = cross.astype(BF16).reshape(NC, ROWS, SEG)
        for dc in range(NC):
            part, there = cov.at[s, p, core(dc)], out_ref.at[:, columns(s, me)]
            if PASSES[p] == 0 and dc == 0:
                pltpu.make_async_copy(part, there, o_local.at[s]).start()
            else:
                k = others.index((PASSES[p], dc))
                send(part, there, o_send.at[s, k], o_recv.at[s, k], here(PASSES[p], dc))

    vpart[...] = jnp.zeros_like(vpart)
    ticks = NZ // 2 + AHEAD * (NY - 1)
    left = {0: [(1, 6), (1, 2), (1, 3)], 1: [(1, 4), (1, 5)], 2: [(1, 0), (1, 1)]}
    ready = False
    for t in range(ticks):
        for p in range(NY):
            step = t - AHEAD * p + 1
            if 1 <= step <= NZ // 2:
                ring_step(step, p)
        for s, k in left.get(t, []):
            pass_over(s, k)
        p, late = divmod(t - (NZ // 2 - 1), AHEAD)
        if 0 <= p < NY and late == 0:
            if not ready:
                gathered(0)
                ready = True
            pass_done(p)
            product(0, p)
    gathered(1)
    for p in range(NY):
        product(1, p)

    v_copy = remote(vpart.at[1 - x], vgot, v_sem.at[0], v_sem.at[1], x_mate)
    v_copy.start()
    for s in range(NX):
        for k, (dy, dc) in enumerate(others):
            k_back = others.index(((NY - dy) % NY, dc))
            there = out_ref.at[:, columns(s, block(dy, dc))]
            remote(cov.at[s, 0, 0], there, o_send.at[s, 0], o_recv.at[s, k_back], here(dy, dc)).wait_recv()
        pltpu.make_async_copy(cov.at[s, 0, 0], out_ref.at[:, columns(s, me)], o_local.at[s]).wait()
    v_copy.wait()
    total = jnp.sum(vpart[x] + vgot[...], axis=0, keepdims=True)
    var_ref[...] = piv_ref[...] - total
    for handle in sends:
        handle.wait_send()


def on_device(ancestor_inverse, factor_block, block_pattern, pivot_inverse):
    rows, wide = factor_block.shape[1:]
    dma = pltpu.SemaphoreType.DMA
    vmem, hbm = pl.BlockSpec(memory_space=pltpu.VMEM), pl.BlockSpec(memory_space=pl.ANY)
    cross_cov, variances = pl.pallas_call(
        kernel,
        out_shape=(
            jax.ShapeDtypeStruct((rows, wide), BF16),
            jax.ShapeDtypeStruct(pivot_inverse.shape, F32),
        ),
        in_specs=[vmem, hbm, pl.BlockSpec(memory_space=pltpu.SMEM), vmem],
        out_specs=(hbm, vmem),
        scratch_shapes=[
            pltpu.VMEM((NX, NY * NC, 2, NX, 64, SEG), BF16),
            pltpu.VMEM((NX, NY * NC, 2, NX, 64, SEG), BF16),
            pltpu.VMEM((NZ, NY, NC, ROWS, 128), BF16),
            pltpu.VMEM((ROWS, 128), BF16),
            pltpu.VMEM((ROWS, 128), BF16),
            pltpu.VMEM((NX, NY, NC, ROWS, SEG), BF16),
            pltpu.VMEM((NX, 8, SEG), F32),
            pltpu.VMEM((8, SEG), F32),
            dma((NX, 7)), dma((NX, 8)), dma((NX, NX, 8)), dma((NX,)),
            dma((2,)), dma((3,)), dma((4,)),
            dma((2, NZ // 2, NY)), dma((2, NZ // 2, NY)),
            dma((NZ, NY)), dma((NZ, NY)),
            dma((NX, 7)), dma((NX, 7)), dma((NX,)), dma((2,)),
        ],
        compiler_params=pltpu.CompilerParams(
            collective_id=0, has_side_effects=True, vmem_limit_bytes=48 << 20
        ),
    )(ancestor_inverse, factor_block.reshape(2, rows // 2, wide), block_pattern, pivot_inverse)
    return cross_cov[None], variances


def solution(mesh):
    return jax.shard_map(
        on_device,
        mesh=mesh,
        in_specs=(P("grid", "leaf"), P("leaf", "grid", None), P("leaf", None), P("leaf", "grid")),
        out_specs=(P("leaf", "grid", None), P("leaf", "grid")),
        check_vma=False,
    )
```

```python
import jax
import jax.numpy as jnp
from jax import lax
from jax.experimental import pallas as pl
from jax.experimental.pallas import tpu as pltpu
from jax.sharding import PartitionSpec as P

MESH = pl.DeviceIdType.MESH
F32, BF16 = jnp.float32, jnp.bfloat16
NX, NY, NC, NZ = 2, 4, 2, 16
ROWS, SEG = 128, 256
CHUNKS = 4
DEEP = 1024
FAR = 4


def kernel(
    a_ref, f_ref, pat_ref, piv_ref, out_ref, var_ref,
    raw, masked, anc, own, packed, cov, vpart, vgot,
    a_sem, s_send, s_recv, l_sem, y_send, y_recv, w_send, w_recv,
    z_send, z_recv, x_send, x_recv, o_send, o_recv, o_local, v_send, v_recv,
):
    leaf, grid = lax.axis_index("leaf"), lax.axis_index("grid")
    xh, z = leaf // NZ, lax.rem(leaf, NZ)
    x, y, c = grid // (NY * NC), lax.rem(grid // NC, NY), lax.rem(grid, NC)
    place_x = xh * NX + x

    def up_y(dy):
        return lax.rem(y + dy, NY)

    def up_z(dz):
        return lax.rem(z + dz + NZ, NZ)

    def other(v, d):
        return lax.rem(v + d, 2)

    def group(dx, dy, dc):
        return (leaf, other(x, dx) * NY * NC + up_y(dy) * NC + other(c, dc))

    def along_z(dz):
        return (xh * NZ + up_z(dz), grid)

    def chip_x(d):
        at = lax.rem(place_x + d, 2 * NX)
        return at // NX, lax.rem(at, NX)

    def along_x(d):
        h, low = chip_x(d)
        return (h * NZ + z, low * NY * NC + y * NC + c)

    core_mate = group(0, 0, 1)
    square = [(0, 1), (1, 0), (1, 1)]
    steps_z = [s * d for d in range(1, FAR + 1) for s in (1, -1)]
    sends = []

    def remote(src, dst, send, recv, to):
        return pltpu.make_async_remote_copy(
            src_ref=src, dst_ref=dst, send_sem=send, recv_sem=recv, device_id=to, device_id_type=MESH
        )

    def send(*copy):
        handle = remote(*copy)
        handle.start()
        sends.append(handle)

    def wait(ref, sem):
        remote(ref, ref, a_sem, sem, core_mate).wait_recv()

    def columns(side, t, cc):
        return pl.ds(pl.multiple_of(((side * NY + t) * NC + cc) * SEG, SEG), SEG)

    a_copy = pltpu.make_async_copy(a_ref, own, a_sem)
    a_copy.start()
    known = [group(dx, 0, dc) for dx, dc in square] + [group(0, dy, 0) for dy in (1, 2, 3)]
    known += [along_x(3 - 2 * xo) for xo in ()] + [along_z(d) for d in steps_z]
    outer = lax.rem(place_x + jnp.where(x == 0, 3, 1), 2 * NX)
    outer_id = ((outer // NX) * NZ + z, lax.rem(outer, NX) * NY * NC + y * NC + c)
    known.append(outer_id)
    barrier = pltpu.get_barrier_semaphore()
    for to in known:
        pl.semaphore_signal(barrier, inc=1, device_id=to, device_id_type=MESH)
    a_copy.wait()
    packed[z] = jnp.concatenate([own[: ROWS // 2], own[ROWS // 2 :]], 1)
    pl.semaphore_wait(barrier, len(known))

    def way(d):
        return (0, d - 1) if d > 0 else (1, -d - 1)

    def send_z(origin, d):
        to = way(d - origin)
        send(packed.at[up_z(origin)], packed.at[up_z(origin)], z_send.at[*to], z_recv.at[*to], along_z(d))

    def wait_z(d):
        wait(packed.at[up_z(-d)], z_recv.at[*way(d)])

    for d in reversed(steps_z):
        send_z(0, d)

    def swap(t):
        mine = raw.at[t, x, y, c]
        for k, (dx, dc) in enumerate(square):
            part = f_ref.at[:, columns(other(x, dx), t, other(c, dc))]
            send(part, mine, s_send.at[t, k], s_recv.at[t, k], group(dx, 0, dc))
        local = pltpu.make_async_copy(f_ref.at[:, columns(x, t, c)], mine, l_sem.at[t])
        local.start()
        return local

    def spread(t, local):
        local.wait()
        for dx in range(NX):
            side = other(x, dx)
            for k, (ddx, dc) in enumerate(square):
                if ddx == dx:
                    wait(raw.at[t, side, y, other(c, dc)], s_recv.at[t, k])
            both = raw.at[t, side, y]
            for k, dy in enumerate((1, 3)):
                send(both, both, y_send.at[t, k, side], y_recv.at[t, k, side], group(0, dy, 0))

    def hand_on(t):
        for k, dy in enumerate((1, 3)):
            for dx in (k, 1 - k):
                part = raw.at[t, dx, up_y(NY - dy)]
                wait(part, y_recv.at[t, k, dx])
                if dx == k:
                    send(part, part, w_send.at[t, k], w_recv.at[t, k], group(0, dy, 0))

    def complete(t):
        for k in range(2):
            wait(raw.at[t, k, up_y(2)], w_recv.at[t, k])

    swaps = [swap(0), swap(1)]
    spread(0, swaps[0])
    swaps.append(swap(2))

    wait_z(FAR)
    for d in range(FAR, 0, -1):
        send_z(-FAR, d)
    wait_z(-FAR)
    for d in range(1 - FAR, 0):
        send_z(FAR, d)

    spread(1, swaps[1])
    swaps.append(swap(3))
    hand_on(0)

    for d in range(1, NZ // 2 + 1):
        for s in (1, -1):
            if d != FAR and s * d != -NZ // 2:
                wait_z(s * d)
    for k in range(NZ // 2):
        even, odd = packed[2 * k], packed[2 * k + 1]
        for half in range(2):
            lanes = slice(half * 64, half * 64 + 64)
            anc[xh, x, c, half * 64 : half * 64 + 64, k * 128 : k * 128 + 128] = jnp.concatenate(
                [even[:, lanes], odd[:, lanes]], 1
            )

    mine = anc.at[xh, x, c]
    for k, d in enumerate((1, 3)):
        send(mine, mine, x_send.at[k], x_recv.at[k], along_x(d))
    send(mine, mine, x_send.at[2], x_recv.at[2], core_mate)

    spread(2, swaps[2])
    hand_on(1)

    for k, d in enumerate((1, 3)):
        h, low = chip_x(2 * NX - d)
        part = anc.at[h, low, c]
        wait(part, x_recv.at[k])
        some = part.at[k * 64 : k * 64 + 64]
        send(some, some, x_send.at[3 + k], x_recv.at[3 + k], along_x(d))
        send(part, part, x_send.at[5 + k], x_recv.at[5 + k], core_mate)
    spread(3, swaps[3])
    h, low = chip_x(2)
    for k in range(2):
        some = anc.at[h, low, c, k * 64 : k * 64 + 64]
        wait(some, x_recv.at[3 + k])
        send(some, some, x_send.at[7 + k], x_recv.at[7 + k], core_mate)
    hand_on(2)
    wait(anc.at[xh, x, other(c, 1)], x_recv.at[2])
    for k, d in enumerate((1, 3)):
        hh, ll = chip_x(2 * NX - d)
        wait(anc.at[hh, ll, other(c, 1)], x_recv.at[5 + k])
    for k in range(2):
        wait(anc.at[h, low, other(c, 1), k * 64 : k * 64 + 64], x_recv.at[7 + k])

    def product(t):
        def keep_block(g, _):
            keep = jnp.full((ROWS, SEG), pat_ref[0, g].astype(F32), F32).astype(BF16)
            side, yy, cc = g // (NY * NC), lax.rem(g // NC, NY), lax.rem(g, NC)
            masked[side, yy, cc] = raw[t, side, yy, cc] * keep
            return 0

        lax.fori_loop(0, NX * NY * NC, keep_block, 0)
        vpart[t] = jnp.zeros((8, SEG), F32)

        def rows_of(i, _):
            side, cc = i // NC, lax.rem(i, NC)
            total = jnp.zeros((ROWS, SEG), F32)
            for k in range(NX):
                total += jnp.dot(anc[k, side, cc], masked[k].reshape(DEEP, SEG), preferred_element_type=F32)
            cross = -total
            terms = masked[side, y, cc].astype(F32) * cross
            vpart[t] += jnp.sum(terms.reshape(ROWS // 8, 8, SEG), axis=0)
            cov[t, side, cc] = cross.astype(BF16)
            return 0

        lax.fori_loop(0, NX * NC, rows_of, 0)
        there = out_ref.at[:, columns(x, t, c)]
        for k, (dx, dc) in enumerate(square):
            part = cov.at[t, other(x, dx), other(c, dc)]
            send(part, there, o_send.at[t, k], o_recv.at[t, k], group(dx, 0, dc))
        pltpu.make_async_copy(cov.at[t, x, c], there, o_local.at[t]).start()

    for t in range(CHUNKS):
        if t == CHUNKS - 1:
            hand_on(t)
        complete(t)
        product(t)

    for k, dy in enumerate((1, 2, 3)):
        send(vpart.at[up_y(dy)], vgot.at[k], v_send.at[k], v_recv.at[k], group(0, dy, 0))
    for t in range(CHUNKS):
        for k, (dx, dc) in enumerate(square):
            wait(out_ref.at[:, columns(other(x, dx), t, other(c, dc))], o_recv.at[t, k])
        there = out_ref.at[:, columns(x, t, c)]
        pltpu.make_async_copy(cov.at[t, x, c], there, o_local.at[t]).wait()
    total = vpart[y]
    for k in range(3):
        wait(vgot.at[k], v_recv.at[k])
        total += vgot[k]
    var_ref[...] = piv_ref[...] - jnp.sum(total, axis=0, keepdims=True)
    for handle in sends:
        handle.wait_send()


def on_device(ancestor_inverse, factor_block, block_pattern, pivot_inverse):
    rows, wide = factor_block.shape[1:]
    dma = pltpu.SemaphoreType.DMA
    vmem, hbm = pl.BlockSpec(memory_space=pltpu.VMEM), pl.BlockSpec(memory_space=pltpu.HBM)
    cross_cov, variances = pl.pallas_call(
        kernel,
        out_shape=(
            jax.ShapeDtypeStruct((rows, wide), BF16),
            jax.ShapeDtypeStruct(pivot_inverse.shape, F32),
        ),
        in_specs=[hbm, hbm, pl.BlockSpec(memory_space=pltpu.SMEM), vmem],
        out_specs=(hbm, vmem),
        scratch_shapes=[
            pltpu.VMEM((CHUNKS, NX, NY, NC, ROWS, SEG), BF16),
            pltpu.VMEM((NX, NY, NC, ROWS, SEG), BF16),
            pltpu.VMEM((2, NX, NC, ROWS, DEEP), BF16),
            pltpu.VMEM((ROWS, 64), BF16),
            pltpu.VMEM((NZ, ROWS // 2, 128), BF16),
            pltpu.VMEM((CHUNKS, NX, NC, ROWS, SEG), BF16),
            pltpu.VMEM((CHUNKS, 8, SEG), F32),
            pltpu.VMEM((3, 8, SEG), F32),
            dma, dma((CHUNKS, 3)), dma((CHUNKS, 3)), dma((CHUNKS,)),
            dma((CHUNKS, 2, 2)), dma((CHUNKS, 2, 2)), dma((CHUNKS, 2)), dma((CHUNKS, 2)),
            dma((2, 8)), dma((2, 8)), dma((9,)), dma((9,)),
            dma((CHUNKS, 3)), dma((CHUNKS, 3)), dma((CHUNKS,)), dma((3,)), dma((3,)),
        ],
        compiler_params=pltpu.CompilerParams(
            collective_id=0, has_side_effects=True, vmem_limit_bytes=48 << 20
        ),
    )(ancestor_inverse, factor_block[0], block_pattern, pivot_inverse)
    return cross_cov[None], variances


def solution(mesh):
    return jax.shard_map(
        on_device,
        mesh=mesh,
        in_specs=(P("grid", "leaf"), P("leaf", "grid", None), P("leaf", None), P("leaf", "grid")),
        out_specs=(P("leaf", "grid", None), P("leaf", "grid")),
        check_vma=False,
    )
```

```python
import jax
import jax.numpy as jnp
from jax import lax
from jax.experimental import pallas as pl
from jax.experimental.pallas import tpu as pltpu
from jax.sharding import PartitionSpec as P

MESH = pl.DeviceIdType.MESH
F32, BF16 = jnp.float32, jnp.bfloat16
NX, NY, NC, NZ = 2, 4, 2, 16
ROWS, SEG = 128, 256
CHUNKS = 4
DEEP = 1024
FAR = 4


def kernel(
    a_ref, f_ref, pat_ref, piv_ref, out_ref, var_ref,
    raw, masked, anc, packed, cov, vpart, vgot,
    hello, a_sem, s_send, s_recv, l_sem, y_send, y_recv, w_send, w_recv,
    z_send, z_recv, x_send, x_recv, o_send, o_recv, o_local, v_send, v_recv,
):
    leaf, grid = lax.axis_index("leaf"), lax.axis_index("grid")
    xh, z = leaf // NZ, lax.rem(leaf, NZ)
    x, y, c = grid // (NY * NC), lax.rem(grid // NC, NY), lax.rem(grid, NC)
    place_x = xh * NX + x

    def up_y(dy):
        return lax.rem(y + dy, NY)

    def up_z(dz):
        return lax.rem(z + dz + NZ, NZ)

    def other(v, d):
        return lax.rem(v + d, 2)

    def group(dx, dy, dc):
        return (leaf, other(x, dx) * NY * NC + up_y(dy) * NC + other(c, dc))

    def along_z(dz):
        return (xh * NZ + up_z(dz), grid)

    def chip_x(d):
        at = lax.rem(place_x + d, 2 * NX)
        return at // NX, lax.rem(at, NX)

    def along_x(d):
        h, low = chip_x(d)
        return (h * NZ + z, low * NY * NC + y * NC + c)

    core_mate = group(0, 0, 1)
    square = [(0, 1), (1, 0), (1, 1)]
    steps_z = [s * d for d in range(1, FAR + 1) for s in (1, -1)]
    sends = []

    def remote(src, dst, send, recv, to):
        return pltpu.make_async_remote_copy(
            src_ref=src, dst_ref=dst, send_sem=send, recv_sem=recv, device_id=to, device_id_type=MESH
        )

    def send(*copy):
        handle = remote(*copy)
        handle.start()
        sends.append(handle)

    def wait(ref, sem):
        remote(ref, ref, a_sem, sem, core_mate).wait_recv()

    def columns(side, t, cc):
        return pl.ds(pl.multiple_of(((side * NY + t) * NC + cc) * SEG, SEG), SEG)

    a_copy = pltpu.make_async_copy(a_ref, packed.at[z], a_sem)
    a_copy.start()
    known = [group(dx, 0, dc) for dx, dc in square] + [group(0, dy, 0) for dy in (1, 2, 3)]
    outer = lax.rem(place_x + jnp.where(x == 0, 3, 1), 2 * NX)
    outer_id = ((outer // NX) * NZ + z, lax.rem(outer, NX) * NY * NC + y * NC + c)
    known.append(outer_id)
    barrier = pltpu.get_barrier_semaphore()
    for to in known:
        pl.semaphore_signal(barrier, inc=1, device_id=to, device_id_type=MESH)
    lower = jnp.int32(0)
    for d in steps_z:
        lower += (up_z(d) < z).astype(jnp.int32)

        @pl.when(up_z(d) > z)
        def _(d=d):
            pl.semaphore_signal(barrier, inc=1, device_id=along_z(d), device_id_type=MESH)

    pl.semaphore_wait(barrier, len(known) + lower)
    for d in steps_z:

        @pl.when(up_z(d) < z)
        def _(d=d):
            pl.semaphore_signal(hello, inc=1, device_id=along_z(d), device_id_type=MESH)

    def way(d):
        return (0, d - 1) if d > 0 else (1, -d - 1)

    def send_z(origin, d):
        to = way(d - origin)
        send(packed.at[up_z(origin)], packed.at[up_z(origin)], z_send.at[*to], z_recv.at[*to], along_z(d))

    def wait_z(d):
        wait(packed.at[up_z(-d)], z_recv.at[*way(d)])

    def swap(t):
        mine = raw.at[t, x, y, c]
        for k, (dx, dc) in enumerate(square):
            part = f_ref.at[:, columns(other(x, dx), t, other(c, dc))]
            send(part, mine, s_send.at[t, k], s_recv.at[t, k], group(dx, 0, dc))
        here = f_ref.at[:, columns(x, t, c)]
        up_and_down(t, here, x, c)
        local = pltpu.make_async_copy(here, mine, l_sem.at[t])
        local.start()
        return local

    def up_and_down(t, src, side, cc):
        for k, dy in enumerate((1, 3)):
            send(src, raw.at[t, side, y, cc], y_send.at[t, k, side, cc], y_recv.at[t, k, side, cc], group(0, dy, 0))

    def spread(t):
        for k, (dx, dc) in enumerate(square):
            side, cc = other(x, dx), other(c, dc)
            part = raw.at[t, side, y, cc]
            wait(part, s_recv.at[t, k])
            up_and_down(t, part, side, cc)

    def hand_on(t):
        for dc in range(NC):
            cc = other(c, dc)
            for dx in range(NX):
                for k, dy in enumerate((1, 3)):
                    side = other(x, dx)
                    part = raw.at[t, side, up_y(NY - dy), cc]
                    wait(part, y_recv.at[t, k, side, cc])

                    @pl.when(side == k)
                    def _(k=k, dy=dy, part=part, cc=cc):
                        remote(part, part, w_send.at[t, k, cc], w_recv.at[t, k, cc], group(0, dy, 0)).start()

    def complete(t):
        for k in range(2):
            for cc in range(NC):
                wait(raw.at[t, k, up_y(2), cc], w_recv.at[t, k, cc])
        locals_[t].wait()

    locals_ = [swap(0), swap(1)]
    spread(0)

    higher = jnp.int32(0)
    for d in steps_z:
        higher += (up_z(d) > z).astype(jnp.int32)
    a_copy.wait()

    @pl.when(higher > 0)
    def _():
        pl.semaphore_wait(hello, higher)

    for d in reversed(steps_z):
        send_z(0, d)
    locals_.append(swap(2))
    spread(1)
    locals_.append(swap(3))

    wait_z(FAR)
    for d in range(FAR, 0, -1):
        send_z(-FAR, d)
    wait_z(-FAR)
    for d in range(1 - FAR, 0):
        send_z(FAR, d)
    spread(2)
    spread(3)

    for d in range(1, NZ // 2 + 1):
        for s in (1, -1):
            if d != FAR and s * d != -NZ // 2:
                wait_z(s * d)
    for k in range(NZ // 2):
        anc[xh, x, c, :, k * 128 : k * 128 + 128] = packed[2 * k : 2 * k + 2].reshape(128, ROWS).T

    mine = anc.at[xh, x, c]
    for k, d in enumerate((1, 3)):
        send(mine, mine, x_send.at[k], x_recv.at[k], along_x(d))
    send(mine, mine, x_send.at[2], x_recv.at[2], core_mate)

    hand_on(0)
    hand_on(1)

    for k, d in enumerate((1, 3)):
        h, low = chip_x(2 * NX - d)
        part = anc.at[h, low, c]
        wait(part, x_recv.at[k])
        some = part.at[k * 64 : k * 64 + 64]
        send(some, some, x_send.at[3 + k], x_recv.at[3 + k], along_x(d))
        send(part, part, x_send.at[5 + k], x_recv.at[5 + k], core_mate)
    hand_on(2)
    hand_on(3)

    def keep(t):
        complete(t)

        def keep_block(g, _):
            one = jnp.full((ROWS, SEG), pat_ref[0, g].astype(F32), F32).astype(BF16)
            side, yy, cc = g // (NY * NC), lax.rem(g // NC, NY), lax.rem(g, NC)
            masked[t, side, yy, cc] = raw[t, side, yy, cc] * one
            return 0

        lax.fori_loop(0, NX * NY * NC, keep_block, 0)

    def product(t, k, dx, dc):
        side, cc = other(x, dx), other(c, dc)
        total = jnp.zeros((ROWS, SEG), F32)
        for h in range(2):
            total += jnp.dot(anc[h, side, cc], masked[t, h].reshape(DEEP, SEG), preferred_element_type=F32)
        cross = -total
        terms = masked[t, side, y, cc].astype(F32) * cross
        vpart[t] += jnp.sum(terms.reshape(ROWS // 8, 8, SEG), axis=0)
        cov[t, side, cc] = cross.astype(BF16)
        there, part = out_ref.at[:, columns(x, t, c)], cov.at[t, side, cc]
        if k is None:
            pltpu.make_async_copy(part, there, o_local.at[t]).start()
        else:
            send(part, there, o_send.at[t, k], o_recv.at[t, k], group(dx, 0, dc))

    def far_rows(t):
        keep(t)
        product(t, 1, 1, 0)
        if t == 0:
            for k, d in enumerate((1, 3)):
                hh, ll = chip_x(2 * NX - d)
                wait(anc.at[hh, ll, other(c, 1)], x_recv.at[5 + k])
        product(t, 2, 1, 1)

    def near_rows(t):
        if t == 0:
            hh, ll = chip_x(2)
            for k in range(2):
                some = anc.at[hh, ll, c, k * 64 : k * 64 + 64]
                wait(some, x_recv.at[3 + k])
                send(some, some, x_send.at[7 + k], x_recv.at[7 + k], core_mate)
            product(t, None, 0, 0)
            wait(anc.at[xh, x, other(c, 1)], x_recv.at[2])
            for k in range(2):
                wait(anc.at[hh, ll, other(c, 1), k * 64 : k * 64 + 64], x_recv.at[7 + k])
            product(t, 0, 0, 1)
        else:
            product(t, 0, 0, 1)
            product(t, None, 0, 0)

    vpart[...] = jnp.zeros_like(vpart)
    far_rows(0)
    far_rows(1)
    near_rows(0)
    far_rows(2)
    near_rows(1)
    far_rows(3)
    near_rows(2)
    near_rows(3)

    for k, dy in enumerate((1, 2, 3)):
        send(vpart.at[up_y(dy)], vgot.at[k], v_send.at[k], v_recv.at[k], group(0, dy, 0))
    for t in range(CHUNKS):
        for k, (dx, dc) in enumerate(square):
            wait(out_ref.at[:, columns(other(x, dx), t, other(c, dc))], o_recv.at[t, k])
        there = out_ref.at[:, columns(x, t, c)]
        pltpu.make_async_copy(cov.at[t, x, c], there, o_local.at[t]).wait()
    total = vpart[y]
    for k in range(3):
        wait(vgot.at[k], v_recv.at[k])
        total += vgot[k]
    var_ref[...] = piv_ref[...] - jnp.sum(total, axis=0, keepdims=True)
    for handle in sends:
        handle.wait_send()
    for t in range(CHUNKS):
        for k in range(2):
            for cc in range(NC):
                part = raw.at[t, k, y, cc]
                remote(part, part, w_send.at[t, k, cc], w_recv.at[t, k, cc], core_mate).wait_send()


def on_device(ancestor_inverse, factor_block, block_pattern, pivot_inverse):
    rows, wide = factor_block.shape[1:]
    dma = pltpu.SemaphoreType.DMA
    vmem, hbm = pl.BlockSpec(memory_space=pltpu.VMEM), pl.BlockSpec(memory_space=pltpu.HBM)
    cross_cov, variances = pl.pallas_call(
        kernel,
        out_shape=(
            jax.ShapeDtypeStruct((rows, wide), BF16),
            jax.ShapeDtypeStruct(pivot_inverse.shape, F32),
        ),
        in_specs=[hbm, hbm, pl.BlockSpec(memory_space=pltpu.SMEM), vmem],
        out_specs=(hbm, vmem),
        scratch_shapes=[
            pltpu.VMEM((CHUNKS, NX, NY, NC, ROWS, SEG), BF16),
            pltpu.VMEM((CHUNKS, NX, NY, NC, ROWS, SEG), BF16),
            pltpu.VMEM((2, NX, NC, ROWS, DEEP), BF16),
            pltpu.VMEM((NZ, 64, ROWS), BF16),
            pltpu.VMEM((CHUNKS, NX, NC, ROWS, SEG), BF16),
            pltpu.VMEM((CHUNKS, 8, SEG), F32),
            pltpu.VMEM((3, 8, SEG), F32),
            pltpu.SemaphoreType.REGULAR, dma, dma((CHUNKS, 3)), dma((CHUNKS, 3)), dma((CHUNKS,)),
            dma((CHUNKS, 2, 2, 2)), dma((CHUNKS, 2, 2, 2)), dma((CHUNKS, 2, 2)), dma((CHUNKS, 2, 2)),
            dma((2, 8)), dma((2, 8)), dma((9,)), dma((9,)),
            dma((CHUNKS, 3)), dma((CHUNKS, 3)), dma((CHUNKS,)), dma((3,)), dma((3,)),
        ],
        compiler_params=pltpu.CompilerParams(
            collective_id=0, has_side_effects=True, vmem_limit_bytes=60 << 20
        ),
    )(ancestor_inverse.T, factor_block[0], block_pattern, pivot_inverse)
    return cross_cov[None], variances


def solution(mesh):
    return jax.shard_map(
        on_device,
        mesh=mesh,
        in_specs=(P("grid", "leaf"), P("leaf", "grid", None), P("leaf", None), P("leaf", "grid")),
        out_specs=(P("leaf", "grid", None), P("leaf", "grid")),
        check_vma=False,
    )
```

```python
import jax
import jax.numpy as jnp
from jax import lax
from jax.experimental import pallas as pl
from jax.experimental.pallas import tpu as pltpu
from jax.sharding import PartitionSpec as P

MESH = pl.DeviceIdType.MESH
F32, BF16 = jnp.float32, jnp.bfloat16
NX, NY, NC, NZ = 2, 4, 2, 16
ROWS, SEG = 128, 256
CHUNKS = 4
DEEP = 1024
FAR = 4


def kernel(
    a_ref, f_ref, pat_in, piv_in, out_ref, var_ref,
    raw, masked, anc, packed, cov, vpart, vgot, pat_ref, piv_ref,
    hello, a_sem, p_sem, s_send, s_recv, l_sem, y_send, y_recv, w_send, w_recv,
    z_send, z_recv, x_send, x_recv, o_send, o_recv, o_local, v_send, v_recv,
):
    leaf, grid = lax.axis_index("leaf"), lax.axis_index("grid")
    xh, z = leaf // NZ, lax.rem(leaf, NZ)
    x, y, c = grid // (NY * NC), lax.rem(grid // NC, NY), lax.rem(grid, NC)
    place_x = xh * NX + x

    def up_y(dy):
        return lax.rem(y + dy, NY)

    def up_z(dz):
        return lax.rem(z + dz + NZ, NZ)

    def other(v, d):
        return lax.rem(v + d, 2)

    def group(dx, dy, dc):
        return (leaf, other(x, dx) * NY * NC + up_y(dy) * NC + other(c, dc))

    def along_z(dz):
        return (xh * NZ + up_z(dz), grid)

    def chip_x(d):
        at = lax.rem(place_x + d, 2 * NX)
        return at // NX, lax.rem(at, NX)

    def along_x(d):
        h, low = chip_x(d)
        return (h * NZ + z, low * NY * NC + y * NC + c)

    core_mate = group(0, 0, 1)
    square = [(0, 1), (1, 0), (1, 1)]
    steps_z = [s * d for d in range(1, FAR + 1) for s in (1, -1)]
    sends = []

    def remote(src, dst, send, recv, to):
        return pltpu.make_async_remote_copy(
            src_ref=src, dst_ref=dst, send_sem=send, recv_sem=recv, device_id=to, device_id_type=MESH
        )

    def send(*copy):
        handle = remote(*copy)
        handle.start()
        sends.append(handle)

    def wait(ref, sem):
        remote(ref, ref, a_sem, sem, core_mate).wait_recv()

    def columns(side, t, cc):
        return pl.ds(pl.multiple_of(((side * NY + t) * NC + cc) * SEG, SEG), SEG)

    a_copy = pltpu.make_async_copy(a_ref, packed.at[z], a_sem)
    a_copy.start()
    small = [
        pltpu.make_async_copy(pat_in, pat_ref, p_sem.at[0]),
        pltpu.make_async_copy(piv_in, piv_ref, p_sem.at[1]),
    ]
    for copy in small:
        copy.start()
    known = [group(dx, 0, dc) for dx, dc in square] + [group(0, dy, 0) for dy in (1, 2, 3)]
    outer = lax.rem(place_x + jnp.where(x == 0, 3, 1), 2 * NX)
    outer_id = ((outer // NX) * NZ + z, lax.rem(outer, NX) * NY * NC + y * NC + c)
    known.append(outer_id)
    barrier = pltpu.get_barrier_semaphore()
    for to in known:
        pl.semaphore_signal(barrier, inc=1, device_id=to, device_id_type=MESH)
    late = z >= NZ // 2
    heard, answers = jnp.int32(0), jnp.int32(0)
    for d in steps_z:
        tells = (up_z(d) > z) | (late & (up_z(d) >= NZ // 2))
        heard += ((up_z(d) < z) | (late & (up_z(d) >= NZ // 2))).astype(jnp.int32)
        answers += ((up_z(d) > z) & jnp.logical_not(late)).astype(jnp.int32)

        @pl.when(tells)
        def _(d=d):
            pl.semaphore_signal(barrier, inc=1, device_id=along_z(d), device_id_type=MESH)

    pl.semaphore_wait(barrier, len(known) + heard)
    for d in steps_z:

        @pl.when((up_z(d) < z) & (up_z(d) < NZ // 2))
        def _(d=d):
            pl.semaphore_signal(hello, inc=1, device_id=along_z(d), device_id_type=MESH)

    def way(d):
        return (0, d - 1) if d > 0 else (1, -d - 1)

    def wait_z(d):
        wait(packed.at[up_z(-d)], z_recv.at[*way(d)])

    def each(low, high, body):
        def step(t, _):
            body(t)
            return 0

        lax.fori_loop(low, high, step, 0)

    def own_copy(t):
        return pltpu.make_async_copy(f_ref.at[:, columns(x, t, c)], raw.at[t, x, y, c], l_sem.at[t])

    def swap_copies(t):
        mine = raw.at[t, x, y, c]
        return [
            remote(
                f_ref.at[:, columns(other(x, dx), t, other(c, dc))],
                mine, s_send.at[t, k], s_recv.at[t, k], group(dx, 0, dc),
            )
            for k, (dx, dc) in enumerate(square)
        ]

    def y_copies(t, src, dx, dc):
        side, cc = other(x, dx), other(c, dc)
        return [
            remote(
                src, raw.at[t, side, y, cc],
                y_send.at[t, k, side, cc], y_recv.at[t, k, side, cc], group(0, dy, 0),
            )
            for k, dy in enumerate((1, 3))
        ]

    def swap(t):
        for copy in y_copies(t, f_ref.at[:, columns(x, t, c)], 0, 0) + swap_copies(t) + [own_copy(t)]:
            copy.start()

    def spread(t):
        for k, (dx, dc) in enumerate(square):
            part = raw.at[t, other(x, dx), y, other(c, dc)]
            wait(part, s_recv.at[t, k])
            for copy in y_copies(t, part, dx, dc):
                copy.start()

    def hand_copy(t, k, cc, at):
        part = raw.at[t, k, at, cc]
        return remote(part, part, w_send.at[t, k, cc], w_recv.at[t, k, cc], group(0, (1, 3)[k], 0))

    def hand_on(t):
        for dc in range(NC):
            cc = other(c, dc)
            for side in range(NX):
                for k in (side, 1 - side):
                    at = up_y(NY - (1, 3)[k])
                    wait(raw.at[t, side, at, cc], y_recv.at[t, k, side, cc])
                    if side == k:
                        hand_copy(t, k, cc, at).start()

    def complete(t):
        for k in range(2):
            for cc in range(NC):
                wait(raw.at[t, k, up_y(2), cc], w_recv.at[t, k, cc])
        own_copy(t).wait()

    def start_z():
        a_copy.wait()
        for d in reversed(steps_z):
            part = packed.at[z]
            remote(part, part, z_send.at[*way(d)], z_recv.at[*way(d)], along_z(d)).start()

    each(0, CHUNKS, swap)

    @pl.when(late)
    def _():
        start_z()

    spread(0)

    @pl.when(jnp.logical_not(late))
    def _():
        pl.semaphore_wait(hello, answers)
        start_z()

    def second_z():
        for far, ds in ((FAR, range(FAR, 0, -1)), (-FAR, range(1 - FAR, 0))):
            wait_z(far)
            for d in ds:
                part, to = packed.at[up_z(-far)], way(d + far)
                remote(part, part, z_send.at[*to], z_recv.at[*to], along_z(d)).start()

    spread(1)
    second_z()
    each(2, CHUNKS, spread)

    for d in range(1, NZ // 2 + 1):
        for s in (1, -1):
            if d != FAR and s * d != -NZ // 2:
                wait_z(s * d)
    for k in range(NZ // 2):
        anc[xh, x, c, :, k * 128 : k * 128 + 128] = packed[2 * k : 2 * k + 2].reshape(128, ROWS).T

    def rows(h, low, cc, half):
        return anc.at[h, low, cc, half * 64 : half * 64 + 64]

    for first in range(2):
        for k, d in enumerate((1, 3)):
            half = (k + first) % 2
            part = rows(xh, x, c, half)
            send(part, part, x_send.at[k, half], x_recv.at[k, half], along_x(d))
    send(anc.at[xh, x, c], anc.at[xh, x, c], x_send.at[2, 0], x_recv.at[2, 0], core_mate)

    each(0, 2, hand_on)

    for first in range(2):
        for k, d in enumerate((1, 3)):
            half = (k + first) % 2
            part = rows(*chip_x(2 * NX - d), c, half)
            wait(part, x_recv.at[k, half])
            if first == 0:
                send(part, part, x_send.at[3, k], x_recv.at[3, k], along_x(d))
            send(part, part, x_send.at[4 + k, half], x_recv.at[4 + k, half], core_mate)
    each(2, CHUNKS, hand_on)

    def keep(t):
        complete(t)

        def keep_block(g):
            one = jnp.full((ROWS, SEG), pat_ref[0, g].astype(F32), F32).astype(BF16)
            side, yy, cc = g // (NY * NC), lax.rem(g // NC, NY), lax.rem(g, NC)
            masked[t, side, yy, cc] = raw[t, side, yy, cc] * one

        each(0, NX * NY * NC, keep_block)

    def result_copy(t, k):
        dx, dc = square[k]
        part, there = cov.at[t, other(x, dx), other(c, dc)], out_ref.at[:, columns(x, t, c)]
        return remote(part, there, o_send.at[t, k], o_recv.at[t, k], group(dx, 0, dc))

    def own_result(t):
        return pltpu.make_async_copy(cov.at[t, x, c], out_ref.at[:, columns(x, t, c)], o_local.at[t])

    def near_ready():
        for k in range(2):
            part = rows(*chip_x(2), c, k)
            wait(part, x_recv.at[3, k])
            remote(part, part, x_send.at[6, k], x_recv.at[6, k], core_mate).start()
        wait(anc.at[xh, x, other(c, 1)], x_recv.at[2, 0])
        for k in range(2):
            wait(rows(*chip_x(2), other(c, 1), k), x_recv.at[6, k])

    def product(i):
        far = (i < 2) | ((lax.rem(i, 2) == 1) & (i < 7))
        t = (i + 1) // 2 - jnp.where(far, 0, 1)
        side = jnp.where(far, 1 - x, x)

        @pl.when(far)
        def _():
            keep(t)

        @pl.when(i == 2)
        def _():
            near_ready()

        total = jnp.zeros((NC * ROWS, SEG), F32)
        for h in range(2):
            total += jnp.dot(
                anc[h, side].reshape(NC * ROWS, DEEP), masked[t, h].reshape(DEEP, SEG), preferred_element_type=F32
            )
        cross = -total
        terms = masked[t, side, y].reshape(NC * ROWS, SEG).astype(F32) * cross
        vpart[t] += jnp.sum(terms.reshape(NC * ROWS // 8, 8, SEG), axis=0)
        cov[t, side] = cross.astype(BF16).reshape(NC, ROWS, SEG)

        @pl.when(far)
        def _():
            result_copy(t, 1).start()
            result_copy(t, 2).start()

        @pl.when(jnp.logical_not(far))
        def _():
            result_copy(t, 0).start()
            own_result(t).start()

    vpart[...] = jnp.zeros_like(vpart)
    for copy in small:
        copy.wait()
    for k, d in enumerate((1, 3)):
        for half in range(2):
            wait(rows(*chip_x(2 * NX - d), other(c, 1), half), x_recv.at[4 + k, half])
    each(0, 2 * CHUNKS, product)

    for k, dy in enumerate((1, 2, 3)):
        send(vpart.at[up_y(dy)], vgot.at[k], v_send.at[k], v_recv.at[k], group(0, dy, 0))

    def results(t):
        for k, (dx, dc) in enumerate(square):
            wait(out_ref.at[:, columns(other(x, dx), t, other(c, dc))], o_recv.at[t, k])
        own_result(t).wait()

    each(0, CHUNKS, results)
    total = vpart[y]
    for k in range(3):
        wait(vgot.at[k], v_recv.at[k])
        total += vgot[k]
    var_ref[...] = piv_ref[...] - jnp.sum(total, axis=0, keepdims=True)
    for handle in sends:
        handle.wait_send()
    for k in range(2):
        remote(rows(xh, x, c, k), rows(xh, x, c, k), x_send.at[6, k], x_recv.at[6, k], core_mate).wait_send()
    for d in range(1 - NZ // 2, NZ // 2 + 1):
        if d:
            remote(packed.at[z], packed.at[z], z_send.at[*way(d)], z_recv.at[*way(d)], core_mate).wait_send()

    def sent(t):
        for copy in swap_copies(t):
            copy.wait_send()
        for dx in range(NX):
            for dc in range(NC):
                for copy in y_copies(t, raw.at[t, x, y, c], dx, dc):
                    copy.wait_send()
        for k in range(2):
            for cc in range(NC):
                hand_copy(t, k, cc, y).wait_send()
        for k in range(3):
            result_copy(t, k).wait_send()

    each(0, CHUNKS, sent)


def hand_over(cross_ref, var_ref, cross_out, var_out, cross, var, sems):
    parts = [pl.ds(k * ROWS // 4, ROWS // 4) for k in range(4)]
    through = [(cross_ref.at[p], cross.at[p], cross_out.at[0, p]) for p in parts] + [(var_ref, var, var_out)]
    loads = [pltpu.make_async_copy(a, b, sems.at[k]) for k, (a, b, _) in enumerate(through)]
    stores = [pltpu.make_async_copy(b, c, sems.at[5 + k]) for k, (_, b, c) in enumerate(through)]
    for load in loads:
        load.start()
    for load, store in zip(loads, stores):
        load.wait()
        store.start()
    for store in stores:
        store.wait()


def on_device(ancestor_inverse, factor_block, block_pattern, pivot_inverse):
    rows, wide = factor_block.shape[1:]
    dma = pltpu.SemaphoreType.DMA
    vmem, hbm = pl.BlockSpec(memory_space=pltpu.VMEM), pl.BlockSpec(memory_space=pltpu.HBM)
    cross_cov, variances = pl.pallas_call(
        kernel,
        out_shape=(
            jax.ShapeDtypeStruct((rows, wide), BF16),
            jax.ShapeDtypeStruct(pivot_inverse.shape, F32),
        ),
        in_specs=[hbm] * 4,
        out_specs=(hbm, vmem),
        scratch_shapes=[
            pltpu.VMEM((CHUNKS, NX, NY, NC, ROWS, SEG), BF16),
            pltpu.VMEM((CHUNKS, NX, NY, NC, ROWS, SEG), BF16),
            pltpu.VMEM((2, NX, NC, ROWS, DEEP), BF16),
            pltpu.VMEM((NZ, 64, ROWS), BF16),
            pltpu.VMEM((CHUNKS, NX, NC, ROWS, SEG), BF16),
            pltpu.VMEM((CHUNKS, 8, SEG), F32),
            pltpu.VMEM((3, 8, SEG), F32),
            pltpu.SMEM(block_pattern.shape, jnp.int32),
            pltpu.VMEM(pivot_inverse.shape, F32),
            pltpu.SemaphoreType.REGULAR, dma, dma((2,)), dma((CHUNKS, 3)), dma((CHUNKS, 3)), dma((CHUNKS,)),
            dma((CHUNKS, 2, 2, 2)), dma((CHUNKS, 2, 2, 2)), dma((CHUNKS, 2, 2)), dma((CHUNKS, 2, 2)),
            dma((2, 8)), dma((2, 8)), dma((7, 2)), dma((7, 2)),
            dma((CHUNKS, 3)), dma((CHUNKS, 3)), dma((CHUNKS,)), dma((3,)), dma((3,)),
        ],
        compiler_params=pltpu.CompilerParams(
            collective_id=0, has_side_effects=True, vmem_limit_bytes=60 << 20
        ),
    )(ancestor_inverse.T, factor_block[0], block_pattern, pivot_inverse)
    return pl.pallas_call(
        hand_over,
        out_shape=(
            jax.ShapeDtypeStruct((1, rows, wide), BF16),
            jax.ShapeDtypeStruct(pivot_inverse.shape, F32),
        ),
        in_specs=[hbm, hbm],
        out_specs=(hbm, hbm),
        scratch_shapes=[pltpu.VMEM((rows, wide), BF16), pltpu.VMEM(pivot_inverse.shape, F32), dma((10,))],
        compiler_params=pltpu.CompilerParams(vmem_limit_bytes=60 << 20),
    )(cross_cov, variances)


def solution(mesh):
    return jax.shard_map(
        on_device,
        mesh=mesh,
        in_specs=(P("grid", "leaf"), P("leaf", "grid", None), P("leaf", None), P("leaf", "grid")),
        out_specs=(P("leaf", "grid", None), P("leaf", "grid")),
        check_vma=False,
    )
```

```python
import jax
import jax.numpy as jnp
from jax import lax
from jax.experimental import pallas as pl
from jax.experimental.pallas import tpu as pltpu
from jax.sharding import PartitionSpec as P

MESH = pl.DeviceIdType.MESH
F32, BF16 = jnp.float32, jnp.bfloat16
NX, NY, NC, NZ = 2, 4, 2, 16
ROWS, SEG = 128, 256
CHUNKS = 4
DEEP = 1024
FAR = 4


def kernel(
    a_ref, f_ref, pat_in, piv_in, out_ref, var_ref,
    raw, masked, anc, packed, cov, vpart, vgot, pat_ref, piv_ref,
    hello, hello0, a_sem, p_sem, s_send, s_recv, l_sem, y_send, y_recv, w_send, w_recv,
    z_send, z_recv, x_send, x_recv, o_send, o_recv, o_local, v_send, v_recv,
):
    leaf, grid = lax.axis_index("leaf"), lax.axis_index("grid")
    xh, z = leaf // NZ, lax.rem(leaf, NZ)
    x, y, c = grid // (NY * NC), lax.rem(grid // NC, NY), lax.rem(grid, NC)
    place_x = xh * NX + x

    def up_y(dy):
        return lax.rem(y + dy, NY)

    def up_z(dz):
        return lax.rem(z + dz + NZ, NZ)

    def other(v, d):
        return lax.rem(v + d, 2)

    def group(dx, dy, dc):
        return (leaf, other(x, dx) * NY * NC + up_y(dy) * NC + other(c, dc))

    def along_z(dz):
        return (xh * NZ + up_z(dz), grid)

    def chip_x(d):
        at = lax.rem(place_x + d, 2 * NX)
        return at // NX, lax.rem(at, NX)

    def along_x(d):
        h, low = chip_x(d)
        return (h * NZ + z, low * NY * NC + y * NC + c)

    core_mate = group(0, 0, 1)
    square = [(0, 1), (1, 0), (1, 1)]
    steps_z = [s * d for d in range(1, FAR + 1) for s in (1, -1)]
    sends = []

    def remote(src, dst, send, recv, to):
        return pltpu.make_async_remote_copy(
            src_ref=src, dst_ref=dst, send_sem=send, recv_sem=recv, device_id=to, device_id_type=MESH
        )

    def send(*copy):
        handle = remote(*copy)
        handle.start()
        sends.append(handle)

    def wait(ref, sem):
        remote(ref, ref, a_sem, sem, core_mate).wait_recv()

    def columns(side, t, cc):
        return pl.ds(pl.multiple_of(((side * NY + t) * NC + cc) * SEG, SEG), SEG)

    a_copy = pltpu.make_async_copy(a_ref, packed.at[z], a_sem)
    a_copy.start()
    small = [
        pltpu.make_async_copy(pat_in, pat_ref, p_sem.at[0]),
        pltpu.make_async_copy(piv_in, piv_ref, p_sem.at[1]),
    ]
    for copy in small:
        copy.start()
    known = [group(dx, 0, dc) for dx, dc in square] + [group(0, dy, 0) for dy in (1, 2, 3)]
    outer = lax.rem(place_x + jnp.where(x == 0, 3, 1), 2 * NX)
    outer_id = ((outer // NX) * NZ + z, lax.rem(outer, NX) * NY * NC + y * NC + c)
    known.append(outer_id)
    barrier = pltpu.get_barrier_semaphore()
    first = (leaf == 0) & (grid == 0)
    square0 = (leaf == 0) & ((grid == 1) | (grid == NY * NC) | (grid == NY * NC + 1))
    row0 = (leaf == 0) & ((grid == NC) | (grid == 2 * NC) | (grid == 3 * NC))
    outer0 = (leaf == NZ) & (grid == NY * NC)
    column0 = (grid == 0) & (leaf >= 1) & (leaf <= FAR)

    def is_first(to):
        return (to[0] == 0) & (to[1] == 0)

    late = z >= NZ // 2

    def rank(v):
        return jnp.where(v < NZ // 2, v, jnp.where(v < 3 * NZ // 4, v + NZ // 4, v - NZ // 4))

    def meets(d):
        return late & (up_z(d) // (NZ // 4) == z // (NZ // 4))

    def above(d):
        return (rank(up_z(d)) > rank(z)) & jnp.logical_not(meets(d))

    def below(d):
        return (rank(up_z(d)) < rank(z)) & jnp.logical_not(meets(d))

    waits = len(known) - (square0 | row0 | outer0).astype(jnp.int32)
    answers = jnp.int32(0)

    @pl.when(jnp.logical_not(first))
    def _():
        for to in known:
            pl.semaphore_signal(barrier, inc=1, device_id=to, device_id_type=MESH)

    def odd_pair(d):
        return (first & (d > 0)) | (column0 & (up_z(d) == 0))

    for d in steps_z:
        tells = (odd_pair(d) & column0) | (jnp.logical_not(odd_pair(d)) & (above(d) | meets(d)))
        hears = (odd_pair(d) & first) | (jnp.logical_not(odd_pair(d)) & (below(d) | meets(d)))
        waits += hears.astype(jnp.int32)
        answers += (above(d) & jnp.logical_not(odd_pair(d))).astype(jnp.int32)

        @pl.when(tells)
        def _(d=d):
            pl.semaphore_signal(barrier, inc=1, device_id=along_z(d), device_id_type=MESH)

    pl.semaphore_wait(barrier, waits)
    for d in steps_z:

        @pl.when(below(d) & jnp.logical_not(odd_pair(d)))
        def _(d=d):
            pl.semaphore_signal(hello, inc=1, device_id=along_z(d), device_id_type=MESH)

    @pl.when(first)
    def _():
        for to in known + [along_z(d) for d in range(1, FAR + 1)]:
            pl.semaphore_signal(hello0, inc=1, device_id=to, device_id_type=MESH)

    def way(d):
        return (0, d - 1) if d > 0 else (1, -d - 1)

    def wait_z(d):
        wait(packed.at[up_z(-d)], z_recv.at[*way(d)])

    def each(low, high, body):
        def step(t, _):
            body(t)
            return 0

        lax.fori_loop(low, high, step, 0)

    def own_copy(t):
        return pltpu.make_async_copy(f_ref.at[:, columns(x, t, c)], raw.at[t, x, y, c], l_sem.at[t])

    def swap_copies(t):
        mine = raw.at[t, x, y, c]
        return [
            remote(
                f_ref.at[:, columns(other(x, dx), t, other(c, dc))],
                mine, s_send.at[t, k], s_recv.at[t, k], group(dx, 0, dc),
            )
            for k, (dx, dc) in enumerate(square)
        ]

    def y_copies(t, src, dx, dc):
        side, cc = other(x, dx), other(c, dc)
        return [
            remote(
                src, raw.at[t, side, y, cc],
                y_send.at[t, k, side, cc], y_recv.at[t, k, side, cc], group(0, dy, 0),
            )
            for k, dy in enumerate((1, 3))
        ]

    neighbours = [group(0, dy, 0) for dy in (1, 3)]
    mates = [group(dx, 0, dc) for dx, dc in square]

    def start(copies, targets, to_first):
        for copy, to in zip(copies, targets):

            @pl.when(is_first(to) == to_first)
            def _(copy=copy):
                copy.start()

    def swap(t, to_first=False):
        start(y_copies(t, f_ref.at[:, columns(x, t, c)], 0, 0), neighbours, to_first)
        start(swap_copies(t), mates, to_first)
        if not to_first:
            own_copy(t).start()

    def spread(t, from_first=False):
        for k, (dx, dc) in enumerate(square):

            @pl.when(is_first(mates[k]) == from_first)
            def _(k=k, dx=dx, dc=dc):
                part = raw.at[t, other(x, dx), y, other(c, dc)]
                wait(part, s_recv.at[t, k])
                start(y_copies(t, part, dx, dc), neighbours, False)

    def spread_to_first(t):
        for dx, dc in square:
            part = raw.at[t, other(x, dx), y, other(c, dc)]
            start(y_copies(t, part, dx, dc), neighbours, True)

    def hand_copy(t, k, cc, at):
        part = raw.at[t, k, at, cc]
        return remote(part, part, w_send.at[t, k, cc], w_recv.at[t, k, cc], group(0, (1, 3)[k], 0))

    def hand_on(t):
        for dc in range(NC):
            cc = other(c, dc)
            for side in range(NX):
                for k in (side, 1 - side):
                    at = up_y(NY - (1, 3)[k])
                    wait(raw.at[t, side, at, cc], y_recv.at[t, k, side, cc])
                    if side == k:
                        hand_copy(t, k, cc, at).start()

    def complete(t):
        for k in range(2):
            for cc in range(NC):
                wait(raw.at[t, k, up_y(2), cc], w_recv.at[t, k, cc])
        own_copy(t).wait()

    def start_z():
        a_copy.wait()
        for d in reversed(steps_z):
            part = packed.at[z]
            remote(part, part, z_send.at[*way(d)], z_recv.at[*way(d)], along_z(d)).start()

    each(0, CHUNKS, swap)

    def rest(t):
        spread(t)

        @pl.when(row0)
        def _():
            spread_to_first(t)

    def second_z():
        for far, ds in ((FAR, range(FAR, 0, -1)), (-FAR, range(1 - FAR, 0))):
            wait_z(far)
            for d in ds:
                part, to = packed.at[up_z(-far)], way(d + far)
                remote(part, part, z_send.at[*to], z_recv.at[*to], along_z(d)).start()

    @pl.when(late)
    def _():
        @pl.when(answers > 0)
        def _():
            pl.semaphore_wait(hello, answers)

        start_z()

    spread(0)

    @pl.when(square0 | row0 | outer0 | column0)
    def _():
        pl.semaphore_wait(hello0, 1)
        each(0, CHUNKS, lambda t: swap(t, True))

        @pl.when(row0)
        def _():
            spread_to_first(0)

    @pl.when(late)
    def _():
        second_z()

    def hello_z():
        pl.semaphore_wait(hello, answers)
        start_z()

    @pl.when((z >= FAR) & (z < NZ // 2))
    def _():
        hello_z()

    rest(1)

    @pl.when((z >= FAR) & (z < NZ // 2))
    def _():
        second_z()

    @pl.when(z < FAR)
    def _():
        hello_z()

    each(2, CHUNKS, rest)

    @pl.when(z < FAR)
    def _():
        second_z()

    @pl.when(square0)
    def _():
        each(0, CHUNKS, lambda t: spread(t, True))


    for d in range(1, NZ // 2 + 1):
        for s in (1, -1):
            if d != FAR and s * d != -NZ // 2:
                wait_z(s * d)
    for k in range(NZ // 2):
        anc[xh, x, c, :, k * 128 : k * 128 + 128] = packed[2 * k : 2 * k + 2].reshape(128, ROWS).T

    def rows(h, low, cc, half):
        return anc.at[h, low, cc, half * 64 : half * 64 + 64]

    for first in range(2):
        for k, d in enumerate((1, 3)):
            half = (k + first) % 2
            part = rows(xh, x, c, half)
            send(part, part, x_send.at[k, half], x_recv.at[k, half], along_x(d))
    send(anc.at[xh, x, c], anc.at[xh, x, c], x_send.at[2, 0], x_recv.at[2, 0], core_mate)

    each(0, 2, hand_on)

    for first in range(2):
        for k, d in enumerate((1, 3)):
            half = (k + first) % 2
            part = rows(*chip_x(2 * NX - d), c, half)
            wait(part, x_recv.at[k, half])
            if first == 0:
                send(part, part, x_send.at[3, k], x_recv.at[3, k], along_x(d))
            send(part, part, x_send.at[4 + k, half], x_recv.at[4 + k, half], core_mate)
    each(2, CHUNKS, hand_on)

    def keep(t):
        complete(t)

        def keep_block(g):
            one = jnp.full((ROWS, SEG), pat_ref[0, g].astype(F32), F32).astype(BF16)
            side, yy, cc = g // (NY * NC), lax.rem(g // NC, NY), lax.rem(g, NC)
            masked[t, side, yy, cc] = raw[t, side, yy, cc] * one

        each(0, NX * NY * NC, keep_block)

    def result_copy(t, k):
        dx, dc = square[k]
        part, there = cov.at[t, other(x, dx), other(c, dc)], out_ref.at[:, columns(x, t, c)]
        return remote(part, there, o_send.at[t, k], o_recv.at[t, k], group(dx, 0, dc))

    def own_result(t):
        return pltpu.make_async_copy(cov.at[t, x, c], out_ref.at[:, columns(x, t, c)], o_local.at[t])

    def near_ready():
        for k in range(2):
            part = rows(*chip_x(2), c, k)
            wait(part, x_recv.at[3, k])
            remote(part, part, x_send.at[6, k], x_recv.at[6, k], core_mate).start()
        wait(anc.at[xh, x, other(c, 1)], x_recv.at[2, 0])
        for k in range(2):
            wait(rows(*chip_x(2), other(c, 1), k), x_recv.at[6, k])

    def product(i):
        far = (i < 2) | ((lax.rem(i, 2) == 1) & (i < 7))
        t = (i + 1) // 2 - jnp.where(far, 0, 1)
        side = jnp.where(far, 1 - x, x)

        @pl.when(far)
        def _():
            keep(t)

        @pl.when(i == 2)
        def _():
            near_ready()

        total = jnp.zeros((NC * ROWS, SEG), F32)
        for h in range(2):
            total += jnp.dot(
                anc[h, side].reshape(NC * ROWS, DEEP), masked[t, h].reshape(DEEP, SEG), preferred_element_type=F32
            )
        cross = -total
        terms = masked[t, side, y].reshape(NC * ROWS, SEG).astype(F32) * cross
        vpart[t] += jnp.sum(terms.reshape(NC * ROWS // 8, 8, SEG), axis=0)
        cov[t, side] = cross.astype(BF16).reshape(NC, ROWS, SEG)

        @pl.when(far)
        def _():
            result_copy(t, 1).start()
            result_copy(t, 2).start()

        @pl.when(jnp.logical_not(far))
        def _():
            result_copy(t, 0).start()
            own_result(t).start()

    vpart[...] = jnp.zeros_like(vpart)
    for copy in small:
        copy.wait()
    for k, d in enumerate((1, 3)):
        for half in range(2):
            wait(rows(*chip_x(2 * NX - d), other(c, 1), half), x_recv.at[4 + k, half])
    each(0, 2 * CHUNKS, product)

    for k, dy in enumerate((1, 2, 3)):
        send(vpart.at[up_y(dy)], vgot.at[k], v_send.at[k], v_recv.at[k], group(0, dy, 0))

    def results(t):
        for k, (dx, dc) in enumerate(square):
            wait(out_ref.at[:, columns(other(x, dx), t, other(c, dc))], o_recv.at[t, k])
        own_result(t).wait()

    each(0, CHUNKS, results)
    total = vpart[y]
    for k in range(3):
        wait(vgot.at[k], v_recv.at[k])
        total += vgot[k]
    var_ref[...] = piv_ref[...] - jnp.sum(total, axis=0, keepdims=True)
    for handle in sends:
        handle.wait_send()
    for k in range(2):
        remote(rows(xh, x, c, k), rows(xh, x, c, k), x_send.at[6, k], x_recv.at[6, k], core_mate).wait_send()
    for d in range(1 - NZ // 2, NZ // 2 + 1):
        if d:
            remote(packed.at[z], packed.at[z], z_send.at[*way(d)], z_recv.at[*way(d)], core_mate).wait_send()

    def sent(t):
        for copy in swap_copies(t):
            copy.wait_send()
        for dx in range(NX):
            for dc in range(NC):
                for copy in y_copies(t, raw.at[t, x, y, c], dx, dc):
                    copy.wait_send()
        for k in range(2):
            for cc in range(NC):
                hand_copy(t, k, cc, y).wait_send()
        for k in range(3):
            result_copy(t, k).wait_send()

    each(0, CHUNKS, sent)


def hand_over(cross_ref, var_ref, cross_out, var_out, cross, var, sems):
    parts = [pl.ds(k * ROWS // 4, ROWS // 4) for k in range(4)]
    through = [(cross_ref.at[p], cross.at[p], cross_out.at[0, p]) for p in parts] + [(var_ref, var, var_out)]
    loads = [pltpu.make_async_copy(a, b, sems.at[k]) for k, (a, b, _) in enumerate(through)]
    stores = [pltpu.make_async_copy(b, c, sems.at[5 + k]) for k, (_, b, c) in enumerate(through)]
    for load in loads:
        load.start()
    for load, store in zip(loads, stores):
        load.wait()
        store.start()
    for store in stores:
        store.wait()


def on_device(ancestor_inverse, factor_block, block_pattern, pivot_inverse):
    rows, wide = factor_block.shape[1:]
    dma = pltpu.SemaphoreType.DMA
    vmem, hbm = pl.BlockSpec(memory_space=pltpu.VMEM), pl.BlockSpec(memory_space=pltpu.HBM)
    cross_cov, variances = pl.pallas_call(
        kernel,
        out_shape=(
            jax.ShapeDtypeStruct((rows, wide), BF16),
            jax.ShapeDtypeStruct(pivot_inverse.shape, F32),
        ),
        in_specs=[hbm] * 4,
        out_specs=(hbm, vmem),
        scratch_shapes=[
            pltpu.VMEM((CHUNKS, NX, NY, NC, ROWS, SEG), BF16),
            pltpu.VMEM((CHUNKS, NX, NY, NC, ROWS, SEG), BF16),
            pltpu.VMEM((2, NX, NC, ROWS, DEEP), BF16),
            pltpu.VMEM((NZ, 64, ROWS), BF16),
            pltpu.VMEM((CHUNKS, NX, NC, ROWS, SEG), BF16),
            pltpu.VMEM((CHUNKS, 8, SEG), F32),
            pltpu.VMEM((3, 8, SEG), F32),
            pltpu.SMEM(block_pattern.shape, jnp.int32),
            pltpu.VMEM(pivot_inverse.shape, F32),
            pltpu.SemaphoreType.REGULAR, pltpu.SemaphoreType.REGULAR, dma, dma((2,)), dma((CHUNKS, 3)), dma((CHUNKS, 3)), dma((CHUNKS,)),
            dma((CHUNKS, 2, 2, 2)), dma((CHUNKS, 2, 2, 2)), dma((CHUNKS, 2, 2)), dma((CHUNKS, 2, 2)),
            dma((2, 8)), dma((2, 8)), dma((7, 2)), dma((7, 2)),
            dma((CHUNKS, 3)), dma((CHUNKS, 3)), dma((CHUNKS,)), dma((3,)), dma((3,)),
        ],
        compiler_params=pltpu.CompilerParams(
            collective_id=0, has_side_effects=True, vmem_limit_bytes=60 << 20
        ),
    )(ancestor_inverse.T, factor_block[0], block_pattern, pivot_inverse)
    return pl.pallas_call(
        hand_over,
        out_shape=(
            jax.ShapeDtypeStruct((1, rows, wide), BF16),
            jax.ShapeDtypeStruct(pivot_inverse.shape, F32),
        ),
        in_specs=[hbm, hbm],
        out_specs=(hbm, hbm),
        scratch_shapes=[pltpu.VMEM((rows, wide), BF16), pltpu.VMEM(pivot_inverse.shape, F32), dma((10,))],
        compiler_params=pltpu.CompilerParams(vmem_limit_bytes=60 << 20),
    )(cross_cov, variances)


def solution(mesh):
    return jax.shard_map(
        on_device,
        mesh=mesh,
        in_specs=(P("grid", "leaf"), P("leaf", "grid", None), P("leaf", None), P("leaf", "grid")),
        out_specs=(P("leaf", "grid", None), P("leaf", "grid")),
        check_vma=False,
    )
```

```python
import jax
import jax.numpy as jnp
from jax import lax
from jax.experimental import pallas as pl
from jax.experimental.pallas import tpu as pltpu
from jax.sharding import PartitionSpec as P

MESH = pl.DeviceIdType.MESH
F32, BF16 = jnp.float32, jnp.bfloat16
NX, NY, NC, NZ = 2, 4, 2, 16
ROWS, SEG = 128, 256
CHUNKS = 4
DEEP = 1024
FAR = 4


def kernel(
    a_ref, f_ref, pat_in, piv_in, out_ref, var_ref,
    raw, masked, anc, packed, cov, vpart, vgot, pat_ref, piv_ref,
    hello, hello0, a_sem, p_sem, s_send, s_recv, l_sem, y_send, y_recv, w_send, w_recv,
    z_send, z_recv, x_send, x_recv, o_send, o_recv, o_local, v_send, v_recv,
):
    leaf, grid = lax.axis_index("leaf"), lax.axis_index("grid")
    xh, z = leaf // NZ, lax.rem(leaf, NZ)
    x, y, c = grid // (NY * NC), lax.rem(grid // NC, NY), lax.rem(grid, NC)
    place_x = xh * NX + x

    def up_y(dy):
        return lax.rem(y + dy, NY)

    def up_z(dz):
        return lax.rem(z + dz + NZ, NZ)

    def other(v, d):
        return lax.rem(v + d, 2)

    def group(dx, dy, dc):
        return (leaf, other(x, dx) * NY * NC + up_y(dy) * NC + other(c, dc))

    def along_z(dz):
        return (xh * NZ + up_z(dz), grid)

    def chip_x(d):
        at = lax.rem(place_x + d, 2 * NX)
        return at // NX, lax.rem(at, NX)

    def along_x(d):
        h, low = chip_x(d)
        return (h * NZ + z, low * NY * NC + y * NC + c)

    core_mate = group(0, 0, 1)
    square = [(0, 1), (1, 0), (1, 1)]
    steps_z = [s * d for d in range(1, FAR + 1) for s in (1, -1)]
    sends = []

    def remote(src, dst, send, recv, to):
        return pltpu.make_async_remote_copy(
            src_ref=src, dst_ref=dst, send_sem=send, recv_sem=recv, device_id=to, device_id_type=MESH
        )

    def send(*copy):
        handle = remote(*copy)
        handle.start()
        sends.append(handle)

    def wait(ref, sem):
        remote(ref, ref, a_sem, sem, core_mate).wait_recv()

    def columns(side, t, cc):
        return pl.ds(pl.multiple_of(((side * NY + t) * NC + cc) * SEG, SEG), SEG)

    a_copy = pltpu.make_async_copy(a_ref, packed.at[z], a_sem)
    a_copy.start()
    small = [
        pltpu.make_async_copy(pat_in, pat_ref, p_sem.at[0]),
        pltpu.make_async_copy(piv_in, piv_ref, p_sem.at[1]),
    ]
    for copy in small:
        copy.start()
    known = [group(dx, 0, dc) for dx, dc in square] + [group(0, dy, 0) for dy in (1, 2, 3)]
    outer = lax.rem(place_x + jnp.where(x == 0, 3, 1), 2 * NX)
    outer_id = ((outer // NX) * NZ + z, lax.rem(outer, NX) * NY * NC + y * NC + c)
    known.append(outer_id)
    barrier = pltpu.get_barrier_semaphore()
    first = (leaf == 0) & (grid == 0)
    square0 = (leaf == 0) & ((grid == 1) | (grid == NY * NC) | (grid == NY * NC + 1))
    row0 = (leaf == 0) & ((grid == NC) | (grid == 2 * NC) | (grid == 3 * NC))
    outer0 = (leaf == NZ) & (grid == NY * NC)
    column0 = (grid == 0) & (leaf >= 1) & (leaf <= FAR)

    def is_first(to):
        return (to[0] == 0) & (to[1] == 0)

    late = z >= NZ // 2

    def rank(v):
        return jnp.where(v < NZ // 2, v, jnp.where(v < 3 * NZ // 4, v + NZ // 4, v - NZ // 4))

    def meets(d):
        return late & (up_z(d) // (NZ // 4) == z // (NZ // 4))

    def above(d):
        return (rank(up_z(d)) > rank(z)) & jnp.logical_not(meets(d))

    def below(d):
        return (rank(up_z(d)) < rank(z)) & jnp.logical_not(meets(d))

    waits = len(known) - (square0 | row0 | outer0).astype(jnp.int32)
    answers = jnp.int32(0)

    @pl.when(jnp.logical_not(first))
    def _():
        for to in known:
            pl.semaphore_signal(barrier, inc=1, device_id=to, device_id_type=MESH)

    def odd_pair(d):
        return (first & (d > 0)) | (column0 & (up_z(d) == 0))

    for d in steps_z:
        tells = (odd_pair(d) & column0) | (jnp.logical_not(odd_pair(d)) & (above(d) | meets(d)))
        hears = (odd_pair(d) & first) | (jnp.logical_not(odd_pair(d)) & (below(d) | meets(d)))
        waits += hears.astype(jnp.int32)
        answers += (above(d) & jnp.logical_not(odd_pair(d))).astype(jnp.int32)

        @pl.when(tells)
        def _(d=d):
            pl.semaphore_signal(barrier, inc=1, device_id=along_z(d), device_id_type=MESH)

    pl.semaphore_wait(barrier, waits)
    for d in steps_z:

        @pl.when(below(d) & jnp.logical_not(odd_pair(d)))
        def _(d=d):
            pl.semaphore_signal(hello, inc=1, device_id=along_z(d), device_id_type=MESH)

    @pl.when(first)
    def _():
        for to in known + [along_z(d) for d in range(1, FAR + 1)]:
            pl.semaphore_signal(hello0, inc=1, device_id=to, device_id_type=MESH)

    def way(d):
        return (0, d - 1) if d > 0 else (1, -d - 1)

    def wait_z(d):
        wait(packed.at[up_z(-d)], z_recv.at[*way(d)])

    def each(low, high, body):
        def step(t, _):
            body(t)
            return 0

        lax.fori_loop(low, high, step, 0)

    def own_copy(t):
        return pltpu.make_async_copy(f_ref.at[:, columns(x, t, c)], raw.at[t, x, y, c], l_sem.at[t])

    def swap_copies(t):
        mine = raw.at[t, x, y, c]
        return [
            remote(
                f_ref.at[:, columns(other(x, dx), t, other(c, dc))],
                mine, s_send.at[t, k], s_recv.at[t, k], group(dx, 0, dc),
            )
            for k, (dx, dc) in enumerate(square)
        ]

    def y_copies(t, src, dx, dc):
        side, cc = other(x, dx), other(c, dc)
        return [
            remote(
                src, raw.at[t, side, y, cc],
                y_send.at[t, k, side, cc], y_recv.at[t, k, side, cc], group(0, dy, 0),
            )
            for k, dy in enumerate((1, 3))
        ]

    neighbours = [group(0, dy, 0) for dy in (1, 3)]
    mates = [group(dx, 0, dc) for dx, dc in square]

    def start(copies, targets, to_first):
        for copy, to in zip(copies, targets):

            @pl.when(is_first(to) == to_first)
            def _(copy=copy):
                copy.start()

    def swap(t, to_first=False):
        start(y_copies(t, f_ref.at[:, columns(x, t, c)], 0, 0), neighbours, to_first)
        start(swap_copies(t), mates, to_first)
        if not to_first:
            own_copy(t).start()

    def spread(t, from_first=False):
        for k, (dx, dc) in enumerate(square):

            @pl.when(is_first(mates[k]) == from_first)
            def _(k=k, dx=dx, dc=dc):
                part = raw.at[t, other(x, dx), y, other(c, dc)]
                wait(part, s_recv.at[t, k])
                start(y_copies(t, part, dx, dc), neighbours, False)

    def spread_to_first(t):
        for dx, dc in square:
            part = raw.at[t, other(x, dx), y, other(c, dc)]
            start(y_copies(t, part, dx, dc), neighbours, True)

    def hand_copy(t, k, cc, at):
        part = raw.at[t, k, at, cc]
        return remote(part, part, w_send.at[t, k, cc], w_recv.at[t, k, cc], group(0, (1, 3)[k], 0))

    def hand_on(t):
        for dc in range(NC):
            cc = other(c, dc)
            for side in range(NX):
                for k in (side, 1 - side):
                    at = up_y(NY - (1, 3)[k])
                    wait(raw.at[t, side, at, cc], y_recv.at[t, k, side, cc])
                    if side == k:
                        hand_copy(t, k, cc, at).start()

    def complete(t):
        for k in range(2):
            for cc in range(NC):
                wait(raw.at[t, k, up_y(2), cc], w_recv.at[t, k, cc])
        own_copy(t).wait()

    def start_z():
        a_copy.wait()
        for d in reversed(steps_z):
            part = packed.at[z]
            remote(part, part, z_send.at[*way(d)], z_recv.at[*way(d)], along_z(d)).start()


    def rest(t):
        spread(t)

        @pl.when(row0)
        def _():
            spread_to_first(t)

    def second_z():
        for far, ds in ((FAR, range(FAR, 0, -1)), (-FAR, range(1 - FAR, 0))):
            wait_z(far)
            for d in ds:
                part, to = packed.at[up_z(-far)], way(d + far)
                remote(part, part, z_send.at[*to], z_recv.at[*to], along_z(d)).start()

    each(0, 1, swap)

    @pl.when(late & (answers == 0))
    def _():
        start_z()

    each(1, CHUNKS, swap)

    @pl.when(late & (answers > 0))
    def _():
        pl.semaphore_wait(hello, answers)
        start_z()

    spread(0)

    @pl.when(square0 | row0 | outer0 | column0)
    def _():
        pl.semaphore_wait(hello0, 1)
        each(0, CHUNKS, lambda t: swap(t, True))

        @pl.when(row0)
        def _():
            spread_to_first(0)

    @pl.when(late)
    def _():
        second_z()

    def hello_z():
        pl.semaphore_wait(hello, answers)
        start_z()

    @pl.when((z >= FAR) & (z < NZ // 2))
    def _():
        hello_z()

    rest(1)

    @pl.when((z >= FAR) & (z < NZ // 2))
    def _():
        second_z()

    @pl.when(z < FAR)
    def _():
        hello_z()

    each(2, CHUNKS, rest)

    @pl.when(z < FAR)
    def _():
        second_z()

    @pl.when(square0)
    def _():
        each(0, CHUNKS, lambda t: spread(t, True))


    for d in range(1, NZ // 2 + 1):
        for s in (1, -1):
            if d != FAR and s * d != -NZ // 2:
                wait_z(s * d)
    for k in range(NZ // 2):
        anc[xh, x, c, :, k * 128 : k * 128 + 128] = packed[2 * k : 2 * k + 2].reshape(128, ROWS).T

    def rows(h, low, cc, half):
        return anc.at[h, low, cc, half * 64 : half * 64 + 64]

    for first in range(2):
        for k, d in enumerate((1, 3)):
            half = (k + first) % 2
            part = rows(xh, x, c, half)
            send(part, part, x_send.at[k, half], x_recv.at[k, half], along_x(d))
    send(anc.at[xh, x, c], anc.at[xh, x, c], x_send.at[2, 0], x_recv.at[2, 0], core_mate)

    each(0, 2, hand_on)

    for first in range(2):
        for k, d in enumerate((1, 3)):
            half = (k + first) % 2
            part = rows(*chip_x(2 * NX - d), c, half)
            wait(part, x_recv.at[k, half])
            if first == 0:
                send(part, part, x_send.at[3, k], x_recv.at[3, k], along_x(d))
            send(part, part, x_send.at[4 + k, half], x_recv.at[4 + k, half], core_mate)
    each(2, CHUNKS, hand_on)

    def keep(t):
        complete(t)

        def keep_block(g):
            one = jnp.full((ROWS, SEG), pat_ref[0, g].astype(F32), F32).astype(BF16)
            side, yy, cc = g // (NY * NC), lax.rem(g // NC, NY), lax.rem(g, NC)
            masked[t, side, yy, cc] = raw[t, side, yy, cc] * one

        each(0, NX * NY * NC, keep_block)

    def result_copy(t, k):
        dx, dc = square[k]
        part, there = cov.at[t, other(x, dx), other(c, dc)], out_ref.at[:, columns(x, t, c)]
        return remote(part, there, o_send.at[t, k], o_recv.at[t, k], group(dx, 0, dc))

    def own_result(t):
        return pltpu.make_async_copy(cov.at[t, x, c], out_ref.at[:, columns(x, t, c)], o_local.at[t])

    def near_ready():
        for k in range(2):
            part = rows(*chip_x(2), c, k)
            wait(part, x_recv.at[3, k])
            remote(part, part, x_send.at[6, k], x_recv.at[6, k], core_mate).start()
        wait(anc.at[xh, x, other(c, 1)], x_recv.at[2, 0])
        for k in range(2):
            wait(rows(*chip_x(2), other(c, 1), k), x_recv.at[6, k])

    def product(i):
        far = (i < 2) | ((lax.rem(i, 2) == 1) & (i < 7))
        t = (i + 1) // 2 - jnp.where(far, 0, 1)
        side = jnp.where(far, 1 - x, x)

        @pl.when(far)
        def _():
            keep(t)

        @pl.when(i == 2)
        def _():
            near_ready()

        total = jnp.zeros((NC * ROWS, SEG), F32)
        for h in range(2):
            total += jnp.dot(
                anc[h, side].reshape(NC * ROWS, DEEP), masked[t, h].reshape(DEEP, SEG), preferred_element_type=F32
            )
        cross = -total
        terms = masked[t, side, y].reshape(NC * ROWS, SEG).astype(F32) * cross
        vpart[t] += jnp.sum(terms.reshape(NC * ROWS // 8, 8, SEG), axis=0)
        cov[t, side] = cross.astype(BF16).reshape(NC, ROWS, SEG)

        @pl.when(far)
        def _():
            result_copy(t, 1).start()
            result_copy(t, 2).start()

        @pl.when(jnp.logical_not(far))
        def _():
            result_copy(t, 0).start()
            own_result(t).start()

    def far_ready():
        for k, d in enumerate((1, 3)):
            for half in range(2):
                wait(rows(*chip_x(2 * NX - d), other(c, 1), half), x_recv.at[4 + k, half])

    def core_rows(cc):
        total = jnp.zeros((ROWS, SEG), F32)
        for h in range(2):
            total += jnp.dot(anc[h, 1 - x, cc], masked[0, h].reshape(DEEP, SEG), preferred_element_type=F32)
        cross = -total
        terms = masked[0, 1 - x, y, cc].astype(F32) * cross
        vpart[0] += jnp.sum(terms.reshape(ROWS // 8, 8, SEG), axis=0)
        cov[0, 1 - x, cc] = cross.astype(BF16)

        @pl.when(cc == c)
        def _():
            result_copy(0, 1).start()

        @pl.when(cc != c)
        def _():
            result_copy(0, 2).start()

    vpart[...] = jnp.zeros_like(vpart)
    for copy in small:
        copy.wait()
    keep(0)
    core_rows(c)
    far_ready()
    core_rows(1 - c)
    each(1, 2 * CHUNKS, product)

    for k, dy in enumerate((1, 2, 3)):
        send(vpart.at[up_y(dy)], vgot.at[k], v_send.at[k], v_recv.at[k], group(0, dy, 0))

    def results(t):
        for k, (dx, dc) in enumerate(square):
            wait(out_ref.at[:, columns(other(x, dx), t, other(c, dc))], o_recv.at[t, k])
        own_result(t).wait()

    each(0, CHUNKS, results)
    total = vpart[y]
    for k in range(3):
        wait(vgot.at[k], v_recv.at[k])
        total += vgot[k]
    var_ref[...] = piv_ref[...] - jnp.sum(total, axis=0, keepdims=True)
    for handle in sends:
        handle.wait_send()
    for k in range(2):
        remote(rows(xh, x, c, k), rows(xh, x, c, k), x_send.at[6, k], x_recv.at[6, k], core_mate).wait_send()
    for d in range(1 - NZ // 2, NZ // 2 + 1):
        if d:
            remote(packed.at[z], packed.at[z], z_send.at[*way(d)], z_recv.at[*way(d)], core_mate).wait_send()

    def sent(t):
        for copy in swap_copies(t):
            copy.wait_send()
        for dx in range(NX):
            for dc in range(NC):
                for copy in y_copies(t, raw.at[t, x, y, c], dx, dc):
                    copy.wait_send()
        for k in range(2):
            for cc in range(NC):
                hand_copy(t, k, cc, y).wait_send()
        for k in range(3):
            result_copy(t, k).wait_send()

    each(0, CHUNKS, sent)


def hand_over(cross_ref, var_ref, cross_out, var_out, cross, var, sems):
    parts = [pl.ds(k * ROWS // 4, ROWS // 4) for k in range(4)]
    through = [(cross_ref.at[p], cross.at[p], cross_out.at[0, p]) for p in parts] + [(var_ref, var, var_out)]
    loads = [pltpu.make_async_copy(a, b, sems.at[k]) for k, (a, b, _) in enumerate(through)]
    stores = [pltpu.make_async_copy(b, c, sems.at[5 + k]) for k, (_, b, c) in enumerate(through)]
    for load in loads:
        load.start()
    for load, store in zip(loads, stores):
        load.wait()
        store.start()
    for store in stores:
        store.wait()


def on_device(ancestor_inverse, factor_block, block_pattern, pivot_inverse):
    rows, wide = factor_block.shape[1:]
    dma = pltpu.SemaphoreType.DMA
    vmem, hbm = pl.BlockSpec(memory_space=pltpu.VMEM), pl.BlockSpec(memory_space=pltpu.HBM)
    cross_cov, variances = pl.pallas_call(
        kernel,
        out_shape=(
            jax.ShapeDtypeStruct((rows, wide), BF16),
            jax.ShapeDtypeStruct(pivot_inverse.shape, F32),
        ),
        in_specs=[hbm] * 4,
        out_specs=(hbm, vmem),
        scratch_shapes=[
            pltpu.VMEM((CHUNKS, NX, NY, NC, ROWS, SEG), BF16),
            pltpu.VMEM((CHUNKS, NX, NY, NC, ROWS, SEG), BF16),
            pltpu.VMEM((2, NX, NC, ROWS, DEEP), BF16),
            pltpu.VMEM((NZ, 64, ROWS), BF16),
            pltpu.VMEM((CHUNKS, NX, NC, ROWS, SEG), BF16),
            pltpu.VMEM((CHUNKS, 8, SEG), F32),
            pltpu.VMEM((3, 8, SEG), F32),
            pltpu.SMEM(block_pattern.shape, jnp.int32),
            pltpu.VMEM(pivot_inverse.shape, F32),
            pltpu.SemaphoreType.REGULAR, pltpu.SemaphoreType.REGULAR, dma, dma((2,)), dma((CHUNKS, 3)), dma((CHUNKS, 3)), dma((CHUNKS,)),
            dma((CHUNKS, 2, 2, 2)), dma((CHUNKS, 2, 2, 2)), dma((CHUNKS, 2, 2)), dma((CHUNKS, 2, 2)),
            dma((2, 8)), dma((2, 8)), dma((7, 2)), dma((7, 2)),
            dma((CHUNKS, 3)), dma((CHUNKS, 3)), dma((CHUNKS,)), dma((3,)), dma((3,)),
        ],
        compiler_params=pltpu.CompilerParams(
            collective_id=0, has_side_effects=True, vmem_limit_bytes=60 << 20
        ),
    )(ancestor_inverse.T, factor_block[0], block_pattern, pivot_inverse)
    return pl.pallas_call(
        hand_over,
        out_shape=(
            jax.ShapeDtypeStruct((1, rows, wide), BF16),
            jax.ShapeDtypeStruct(pivot_inverse.shape, F32),
        ),
        in_specs=[hbm, hbm],
        out_specs=(hbm, hbm),
        scratch_shapes=[pltpu.VMEM((rows, wide), BF16), pltpu.VMEM(pivot_inverse.shape, F32), dma((10,))],
        compiler_params=pltpu.CompilerParams(vmem_limit_bytes=60 << 20),
    )(cross_cov, variances)


def solution(mesh):
    return jax.shard_map(
        on_device,
        mesh=mesh,
        in_specs=(P("grid", "leaf"), P("leaf", "grid", None), P("leaf", None), P("leaf", "grid")),
        out_specs=(P("leaf", "grid", None), P("leaf", "grid")),
        check_vma=False,
    )
```

```python
import jax
import jax.numpy as jnp
from jax import lax
from jax.experimental import pallas as pl
from jax.experimental.pallas import tpu as pltpu
from jax.sharding import PartitionSpec as P

MESH = pl.DeviceIdType.MESH
F32, BF16 = jnp.float32, jnp.bfloat16
NX, NY, NC, NZ = 2, 4, 2, 16
ROWS, SEG = 128, 256
CHUNKS = 4
DEEP = 1024
FAR = 4


def kernel(
    a_ref, f_ref, pat_in, piv_in, out_ref, var_ref,
    raw, masked, anc, packed, cov, vpart, vgot, pat_ref, piv_ref,
    hello, hello0, a_sem, p_sem, s_send, s_recv, l_sem, y_send, y_recv, w_send, w_recv,
    z_send, z_recv, x_send, x_recv, o_send, o_recv, o_local, v_send, v_recv,
):
    leaf, grid = lax.axis_index("leaf"), lax.axis_index("grid")
    xh, z = leaf // NZ, lax.rem(leaf, NZ)
    x, y, c = grid // (NY * NC), lax.rem(grid // NC, NY), lax.rem(grid, NC)
    place_x = xh * NX + x

    def up_y(dy):
        return lax.rem(y + dy, NY)

    def up_z(dz):
        return lax.rem(z + dz + NZ, NZ)

    def other(v, d):
        return lax.rem(v + d, 2)

    def group(dx, dy, dc):
        return (leaf, other(x, dx) * NY * NC + up_y(dy) * NC + other(c, dc))

    def along_z(dz):
        return (xh * NZ + up_z(dz), grid)

    def chip_x(d):
        at = lax.rem(place_x + d, 2 * NX)
        return at // NX, lax.rem(at, NX)

    def along_x(d):
        h, low = chip_x(d)
        return (h * NZ + z, low * NY * NC + y * NC + c)

    core_mate = group(0, 0, 1)
    square = [(0, 1), (1, 0), (1, 1)]
    steps_z = [s * d for d in range(1, FAR + 1) for s in (1, -1)]
    sends = []

    def remote(src, dst, send, recv, to):
        return pltpu.make_async_remote_copy(
            src_ref=src, dst_ref=dst, send_sem=send, recv_sem=recv, device_id=to, device_id_type=MESH
        )

    def send(*copy):
        handle = remote(*copy)
        handle.start()
        sends.append(handle)

    def wait(ref, sem):
        remote(ref, ref, a_sem, sem, core_mate).wait_recv()

    def columns(side, t, cc):
        return pl.ds(pl.multiple_of(((side * NY + t) * NC + cc) * SEG, SEG), SEG)

    a_copy = pltpu.make_async_copy(a_ref, packed.at[z], a_sem)
    a_copy.start()
    small = [
        pltpu.make_async_copy(pat_in, pat_ref, p_sem.at[0]),
        pltpu.make_async_copy(piv_in, piv_ref, p_sem.at[1]),
    ]
    for copy in small:
        copy.start()
    known = [group(dx, 0, dc) for dx, dc in square] + [group(0, dy, 0) for dy in (1, 2, 3)]
    outer = lax.rem(place_x + jnp.where(x == 0, 3, 1), 2 * NX)
    outer_id = ((outer // NX) * NZ + z, lax.rem(outer, NX) * NY * NC + y * NC + c)
    known.append(outer_id)
    barrier = pltpu.get_barrier_semaphore()
    first = (leaf == 0) & (grid == 0)
    square0 = (leaf == 0) & ((grid == 1) | (grid == NY * NC) | (grid == NY * NC + 1))
    row0 = (leaf == 0) & ((grid == NC) | (grid == 2 * NC) | (grid == 3 * NC))
    outer0 = (leaf == NZ) & (grid == NY * NC)
    column0 = (grid == 0) & (leaf >= 1) & (leaf <= FAR)

    def is_first(to):
        return (to[0] == 0) & (to[1] == 0)

    late = z >= NZ // 2

    def rank(v):
        return jnp.where(v < NZ // 2, v, jnp.where(v < 3 * NZ // 4, v + NZ // 4, v - NZ // 4))

    def meets(d):
        return late & (up_z(d) // (NZ // 4) == z // (NZ // 4))

    def above(d):
        return (rank(up_z(d)) > rank(z)) & jnp.logical_not(meets(d))

    def below(d):
        return (rank(up_z(d)) < rank(z)) & jnp.logical_not(meets(d))

    waits = len(known) - (square0 | row0 | outer0).astype(jnp.int32)
    answers = jnp.int32(0)

    @pl.when(jnp.logical_not(first))
    def _():
        for to in known:
            pl.semaphore_signal(barrier, inc=1, device_id=to, device_id_type=MESH)

    def odd_pair(d):
        return (first & (d > 0)) | (column0 & (up_z(d) == 0))

    for d in steps_z:
        tells = (odd_pair(d) & column0) | (jnp.logical_not(odd_pair(d)) & (above(d) | meets(d)))
        hears = (odd_pair(d) & first) | (jnp.logical_not(odd_pair(d)) & (below(d) | meets(d)))
        waits += hears.astype(jnp.int32)
        answers += (above(d) & jnp.logical_not(odd_pair(d))).astype(jnp.int32)

        @pl.when(tells)
        def _(d=d):
            pl.semaphore_signal(barrier, inc=1, device_id=along_z(d), device_id_type=MESH)

    pl.semaphore_wait(barrier, waits)
    for d in steps_z:

        @pl.when(below(d) & jnp.logical_not(odd_pair(d)))
        def _(d=d):
            pl.semaphore_signal(hello, inc=1, device_id=along_z(d), device_id_type=MESH)

    @pl.when(first)
    def _():
        for to in known + [along_z(d) for d in range(1, FAR + 1)]:
            pl.semaphore_signal(hello0, inc=1, device_id=to, device_id_type=MESH)

    def way(d):
        return (0, d - 1) if d > 0 else (1, -d - 1)

    def wait_z(d):
        wait(packed.at[up_z(-d)], z_recv.at[*way(d)])

    def each(low, high, body):
        def step(t, _):
            body(t)
            return 0

        lax.fori_loop(low, high, step, 0)

    def own_copy(t):
        return pltpu.make_async_copy(f_ref.at[:, columns(x, t, c)], raw.at[t, x, y, c], l_sem.at[t])

    def swap_copies(t):
        mine = raw.at[t, x, y, c]
        return [
            remote(
                f_ref.at[:, columns(other(x, dx), t, other(c, dc))],
                mine, s_send.at[t, k], s_recv.at[t, k], group(dx, 0, dc),
            )
            for k, (dx, dc) in enumerate(square)
        ]

    def y_copies(t, src, dx, dc):
        side, cc = other(x, dx), other(c, dc)
        return [
            remote(
                src, raw.at[t, side, y, cc],
                y_send.at[t, k, side, cc], y_recv.at[t, k, side, cc], group(0, dy, 0),
            )
            for k, dy in enumerate((1, 3))
        ]

    neighbours = [group(0, dy, 0) for dy in (1, 3)]
    mates = [group(dx, 0, dc) for dx, dc in square]

    def start(copies, targets, to_first):
        for copy, to in zip(copies, targets):

            @pl.when(is_first(to) == to_first)
            def _(copy=copy):
                copy.start()

    def swap(t, to_first=False):
        start(y_copies(t, f_ref.at[:, columns(x, t, c)], 0, 0), neighbours, to_first)
        start(swap_copies(t), mates, to_first)
        if not to_first:
            own_copy(t).start()

    def spread(t, from_first=False):
        for k, (dx, dc) in enumerate(square):

            @pl.when(is_first(mates[k]) == from_first)
            def _(k=k, dx=dx, dc=dc):
                part = raw.at[t, other(x, dx), y, other(c, dc)]
                wait(part, s_recv.at[t, k])
                start(y_copies(t, part, dx, dc), neighbours, False)

    def spread_to_first(t):
        for dx, dc in square:
            part = raw.at[t, other(x, dx), y, other(c, dc)]
            start(y_copies(t, part, dx, dc), neighbours, True)

    def hand_copy(t, k, cc, at):
        part = raw.at[t, k, at, cc]
        return remote(part, part, w_send.at[t, k, cc], w_recv.at[t, k, cc], group(0, (1, 3)[k], 0))

    def hand_on(t):
        for dc in range(NC):
            cc = other(c, dc)
            for side in range(NX):
                for k in (side, 1 - side):
                    at = up_y(NY - (1, 3)[k])
                    wait(raw.at[t, side, at, cc], y_recv.at[t, k, side, cc])
                    if side == k:
                        hand_copy(t, k, cc, at).start()

    def complete(t):
        for k in range(2):
            for cc in range(NC):
                wait(raw.at[t, k, up_y(2), cc], w_recv.at[t, k, cc])
        own_copy(t).wait()

    def start_z():
        a_copy.wait()
        for d in reversed(steps_z):
            part = packed.at[z]
            remote(part, part, z_send.at[*way(d)], z_recv.at[*way(d)], along_z(d)).start()


    def rest(t):
        spread(t)

        @pl.when(row0)
        def _():
            spread_to_first(t)

    def second_z():
        for far, ds in ((FAR, range(FAR, 0, -1)), (-FAR, range(1 - FAR, 0))):
            wait_z(far)
            for d in ds:
                part, to = packed.at[up_z(-far)], way(d + far)
                remote(part, part, z_send.at[*to], z_recv.at[*to], along_z(d)).start()

    each(0, 1, swap)

    @pl.when(late & (answers == 0))
    def _():
        start_z()

    each(1, CHUNKS, swap)

    @pl.when(late & (answers > 0))
    def _():
        pl.semaphore_wait(hello, answers)
        start_z()

    spread(0)

    @pl.when(square0 | row0 | outer0 | column0)
    def _():
        pl.semaphore_wait(hello0, 1)
        each(0, CHUNKS, lambda t: swap(t, True))

        @pl.when(row0)
        def _():
            spread_to_first(0)

    @pl.when(late)
    def _():
        second_z()

    def hello_z():
        pl.semaphore_wait(hello, answers)
        start_z()

    @pl.when((z >= FAR) & (z < NZ // 2))
    def _():
        hello_z()

    rest(1)

    @pl.when((z >= FAR) & (z < NZ // 2))
    def _():
        second_z()

    @pl.when(z < FAR)
    def _():
        hello_z()

    each(2, CHUNKS, rest)

    @pl.when(z < FAR)
    def _():
        second_z()

    @pl.when(square0)
    def _():
        each(0, CHUNKS, lambda t: spread(t, True))


    for d in range(1, NZ // 2 + 1):
        for s in (1, -1):
            if d != FAR and s * d != -NZ // 2:
                wait_z(s * d)
    for k in range(NZ // 2):
        anc[xh, x, c, :, k * 128 : k * 128 + 128] = packed[2 * k : 2 * k + 2].reshape(128, ROWS).T

    def rows(h, low, cc, half):
        return anc.at[h, low, cc, half * 64 : half * 64 + 64]

    for first in range(2):
        for k, d in enumerate((1, 3)):
            half = (k + first) % 2
            part = rows(xh, x, c, half)
            send(part, part, x_send.at[k, half], x_recv.at[k, half], along_x(d))
    send(anc.at[xh, x, c], anc.at[xh, x, c], x_send.at[2, 0], x_recv.at[2, 0], core_mate)

    each(0, 2, hand_on)

    for first in range(2):
        for k, d in enumerate((1, 3)):
            half = (k + first) % 2
            part = rows(*chip_x(2 * NX - d), c, half)
            wait(part, x_recv.at[k, half])
            if first == 0:
                send(part, part, x_send.at[3, k], x_recv.at[3, k], along_x(d))
            send(part, part, x_send.at[4 + k, half], x_recv.at[4 + k, half], core_mate)
    each(2, CHUNKS, hand_on)

    def keep(t):
        complete(t)

        def keep_block(g):
            one = jnp.full((ROWS, SEG), pat_ref[0, g].astype(F32), F32).astype(BF16)
            side, yy, cc = g // (NY * NC), lax.rem(g // NC, NY), lax.rem(g, NC)
            masked[t, side, yy, cc] = raw[t, side, yy, cc] * one

        each(0, NX * NY * NC, keep_block)

    def result_copy(t, k):
        dx, dc = square[k]
        part, there = cov.at[t, other(x, dx), other(c, dc)], out_ref.at[:, columns(x, t, c)]
        return remote(part, there, o_send.at[t, k], o_recv.at[t, k], group(dx, 0, dc))

    def own_result(t):
        return pltpu.make_async_copy(cov.at[t, x, c], out_ref.at[:, columns(x, t, c)], o_local.at[t])

    def near_forward():
        for k in range(2):
            part = rows(*chip_x(2), c, k)
            wait(part, x_recv.at[3, k])
            remote(part, part, x_send.at[6, k], x_recv.at[6, k], core_mate).start()

    def near_ready():
        wait(anc.at[xh, x, other(c, 1)], x_recv.at[2, 0])
        for k in range(2):
            wait(rows(*chip_x(2), other(c, 1), k), x_recv.at[6, k])

    def product(i):
        far = (i < 3) | (i == 5)
        t = jnp.where(i < 3, i, jnp.where(i < 5, i - 3, jnp.where(i == 5, 3, i - 4)))
        side = jnp.where(far, 1 - x, x)

        @pl.when(i == 2)
        def _():
            near_forward()

        @pl.when(far)
        def _():
            keep(t)

        @pl.when(i == 3)
        def _():
            near_ready()

        total = jnp.zeros((NC * ROWS, SEG), F32)
        for h in range(2):
            total += jnp.dot(
                anc[h, side].reshape(NC * ROWS, DEEP), masked[t, h].reshape(DEEP, SEG), preferred_element_type=F32
            )
        cross = -total
        terms = masked[t, side, y].reshape(NC * ROWS, SEG).astype(F32) * cross
        vpart[t] += jnp.sum(terms.reshape(NC * ROWS // 8, 8, SEG), axis=0)
        cov[t, side] = cross.astype(BF16).reshape(NC, ROWS, SEG)

        @pl.when(far)
        def _():
            result_copy(t, 1).start()
            result_copy(t, 2).start()

        @pl.when(jnp.logical_not(far))
        def _():
            result_copy(t, 0).start()
            own_result(t).start()

    def far_ready():
        for k, d in enumerate((1, 3)):
            for half in range(2):
                wait(rows(*chip_x(2 * NX - d), other(c, 1), half), x_recv.at[4 + k, half])

    def core_rows(cc):
        total = jnp.zeros((ROWS, SEG), F32)
        for h in range(2):
            total += jnp.dot(anc[h, 1 - x, cc], masked[0, h].reshape(DEEP, SEG), preferred_element_type=F32)
        cross = -total
        terms = masked[0, 1 - x, y, cc].astype(F32) * cross
        vpart[0] += jnp.sum(terms.reshape(ROWS // 8, 8, SEG), axis=0)
        cov[0, 1 - x, cc] = cross.astype(BF16)

        @pl.when(cc == c)
        def _():
            result_copy(0, 1).start()

        @pl.when(cc != c)
        def _():
            result_copy(0, 2).start()

    vpart[...] = jnp.zeros_like(vpart)
    for copy in small:
        copy.wait()
    keep(0)
    core_rows(c)
    far_ready()
    core_rows(1 - c)
    each(1, 2 * CHUNKS, product)

    for k, dy in enumerate((1, 2, 3)):
        send(vpart.at[up_y(dy)], vgot.at[k], v_send.at[k], v_recv.at[k], group(0, dy, 0))

    def results(t):
        for k, (dx, dc) in enumerate(square):
            wait(out_ref.at[:, columns(other(x, dx), t, other(c, dc))], o_recv.at[t, k])
        own_result(t).wait()

    each(0, CHUNKS, results)
    total = vpart[y]
    for k in range(3):
        wait(vgot.at[k], v_recv.at[k])
        total += vgot[k]
    var_ref[...] = piv_ref[...] - jnp.sum(total, axis=0, keepdims=True)
    for handle in sends:
        handle.wait_send()
    for k in range(2):
        remote(rows(xh, x, c, k), rows(xh, x, c, k), x_send.at[6, k], x_recv.at[6, k], core_mate).wait_send()
    for d in range(1 - NZ // 2, NZ // 2 + 1):
        if d:
            remote(packed.at[z], packed.at[z], z_send.at[*way(d)], z_recv.at[*way(d)], core_mate).wait_send()

    def sent(t):
        for copy in swap_copies(t):
            copy.wait_send()
        for dx in range(NX):
            for dc in range(NC):
                for copy in y_copies(t, raw.at[t, x, y, c], dx, dc):
                    copy.wait_send()
        for k in range(2):
            for cc in range(NC):
                hand_copy(t, k, cc, y).wait_send()
        for k in range(3):
            result_copy(t, k).wait_send()

    each(0, CHUNKS, sent)


def hand_over(cross_ref, var_ref, cross_out, var_out, cross, var, sems):
    parts = [pl.ds(k * ROWS // 4, ROWS // 4) for k in range(4)]
    through = [(cross_ref.at[p], cross.at[p], cross_out.at[0, p]) for p in parts] + [(var_ref, var, var_out)]
    loads = [pltpu.make_async_copy(a, b, sems.at[k]) for k, (a, b, _) in enumerate(through)]
    stores = [pltpu.make_async_copy(b, c, sems.at[5 + k]) for k, (_, b, c) in enumerate(through)]
    for load in loads:
        load.start()
    for load, store in zip(loads, stores):
        load.wait()
        store.start()
    for store in stores:
        store.wait()


def on_device(ancestor_inverse, factor_block, block_pattern, pivot_inverse):
    rows, wide = factor_block.shape[1:]
    dma = pltpu.SemaphoreType.DMA
    vmem, hbm = pl.BlockSpec(memory_space=pltpu.VMEM), pl.BlockSpec(memory_space=pltpu.HBM)
    cross_cov, variances = pl.pallas_call(
        kernel,
        out_shape=(
            jax.ShapeDtypeStruct((rows, wide), BF16),
            jax.ShapeDtypeStruct(pivot_inverse.shape, F32),
        ),
        in_specs=[hbm] * 4,
        out_specs=(hbm, vmem),
        scratch_shapes=[
            pltpu.VMEM((CHUNKS, NX, NY, NC, ROWS, SEG), BF16),
            pltpu.VMEM((CHUNKS, NX, NY, NC, ROWS, SEG), BF16),
            pltpu.VMEM((2, NX, NC, ROWS, DEEP), BF16),
            pltpu.VMEM((NZ, 64, ROWS), BF16),
            pltpu.VMEM((CHUNKS, NX, NC, ROWS, SEG), BF16),
            pltpu.VMEM((CHUNKS, 8, SEG), F32),
            pltpu.VMEM((3, 8, SEG), F32),
            pltpu.SMEM(block_pattern.shape, jnp.int32),
            pltpu.VMEM(pivot_inverse.shape, F32),
            pltpu.SemaphoreType.REGULAR, pltpu.SemaphoreType.REGULAR, dma, dma((2,)), dma((CHUNKS, 3)), dma((CHUNKS, 3)), dma((CHUNKS,)),
            dma((CHUNKS, 2, 2, 2)), dma((CHUNKS, 2, 2, 2)), dma((CHUNKS, 2, 2)), dma((CHUNKS, 2, 2)),
            dma((2, 8)), dma((2, 8)), dma((7, 2)), dma((7, 2)),
            dma((CHUNKS, 3)), dma((CHUNKS, 3)), dma((CHUNKS,)), dma((3,)), dma((3,)),
        ],
        compiler_params=pltpu.CompilerParams(
            collective_id=0, has_side_effects=True, vmem_limit_bytes=60 << 20
        ),
    )(ancestor_inverse.T, factor_block[0], block_pattern, pivot_inverse)
    return pl.pallas_call(
        hand_over,
        out_shape=(
            jax.ShapeDtypeStruct((1, rows, wide), BF16),
            jax.ShapeDtypeStruct(pivot_inverse.shape, F32),
        ),
        in_specs=[hbm, hbm],
        out_specs=(hbm, hbm),
        scratch_shapes=[pltpu.VMEM((rows, wide), BF16), pltpu.VMEM(pivot_inverse.shape, F32), dma((10,))],
        compiler_params=pltpu.CompilerParams(vmem_limit_bytes=60 << 20),
    )(cross_cov, variances)


def solution(mesh):
    return jax.shard_map(
        on_device,
        mesh=mesh,
        in_specs=(P("grid", "leaf"), P("leaf", "grid", None), P("leaf", None), P("leaf", "grid")),
        out_specs=(P("leaf", "grid", None), P("leaf", "grid")),
        check_vma=False,
    )
```

```python
import jax
import jax.numpy as jnp
from jax import lax
from jax.experimental import pallas as pl
from jax.experimental.pallas import tpu as pltpu
from jax.sharding import PartitionSpec as P

MESH = pl.DeviceIdType.MESH
F32, BF16 = jnp.float32, jnp.bfloat16
NX, NY, NC, NZ = 2, 4, 2, 16
ROWS, SEG = 128, 256
CHUNKS = 4
DEEP = 1024
FAR = 4


def kernel(
    a_ref, f_ref, pat_in, piv_in, out_ref, var_ref,
    raw, masked, anc, packed, cov, vpart, vgot, pat_ref, piv_ref,
    hello, hello0, a_sem, p_sem, s_send, s_recv, l_sem, y_send, y_recv, w_send, w_recv,
    z_send, z_recv, x_send, x_recv, o_send, o_recv, o_local, v_send, v_recv,
):
    leaf, grid = lax.axis_index("leaf"), lax.axis_index("grid")
    xh, z = leaf // NZ, lax.rem(leaf, NZ)
    x, y, c = grid // (NY * NC), lax.rem(grid // NC, NY), lax.rem(grid, NC)
    place_x = xh * NX + x

    def up_y(dy):
        return lax.rem(y + dy, NY)

    def up_z(dz):
        return lax.rem(z + dz + NZ, NZ)

    def other(v, d):
        return lax.rem(v + d, 2)

    def group(dx, dy, dc):
        return (leaf, other(x, dx) * NY * NC + up_y(dy) * NC + other(c, dc))

    def along_z(dz):
        return (xh * NZ + up_z(dz), grid)

    def chip_x(d):
        at = lax.rem(place_x + d, 2 * NX)
        return at // NX, lax.rem(at, NX)

    def along_x(d):
        h, low = chip_x(d)
        return (h * NZ + z, low * NY * NC + y * NC + c)

    core_mate = group(0, 0, 1)
    square = [(0, 1), (1, 0), (1, 1)]
    steps_z = [s * d for d in range(1, FAR + 1) for s in (1, -1)]
    sends = []

    def remote(src, dst, send, recv, to):
        return pltpu.make_async_remote_copy(
            src_ref=src, dst_ref=dst, send_sem=send, recv_sem=recv, device_id=to, device_id_type=MESH
        )

    def send(*copy):
        handle = remote(*copy)
        handle.start()
        sends.append(handle)

    def wait(ref, sem):
        remote(ref, ref, a_sem, sem, core_mate).wait_recv()

    def columns(side, t, cc):
        return pl.ds(pl.multiple_of(((side * NY + t) * NC + cc) * SEG, SEG), SEG)

    a_copy = pltpu.make_async_copy(a_ref, packed.at[z], a_sem)
    a_copy.start()
    small = [
        pltpu.make_async_copy(pat_in, pat_ref, p_sem.at[0]),
        pltpu.make_async_copy(piv_in, piv_ref, p_sem.at[1]),
    ]
    for copy in small:
        copy.start()
    known = [group(dx, 0, dc) for dx, dc in square] + [group(0, dy, 0) for dy in (1, 2, 3)]
    outer = lax.rem(place_x + jnp.where(x == 0, 3, 1), 2 * NX)
    outer_id = ((outer // NX) * NZ + z, lax.rem(outer, NX) * NY * NC + y * NC + c)
    known.append(outer_id)
    barrier = pltpu.get_barrier_semaphore()
    first = (leaf == 0) & (grid == 0)
    square0 = (leaf == 0) & ((grid == 1) | (grid == NY * NC) | (grid == NY * NC + 1))
    row0 = (leaf == 0) & ((grid == NC) | (grid == 2 * NC) | (grid == 3 * NC))
    outer0 = (leaf == NZ) & (grid == NY * NC)
    column0 = (grid == 0) & (leaf >= 1) & (leaf <= FAR)

    def is_first(to):
        return (to[0] == 0) & (to[1] == 0)

    late = z >= NZ // 2

    def rank(v):
        return jnp.where(v < NZ // 2, v, jnp.where(v < 3 * NZ // 4, v + NZ // 4, v - NZ // 4))

    def meets(d):
        return late & (up_z(d) // (NZ // 4) == z // (NZ // 4))

    def above(d):
        return (rank(up_z(d)) > rank(z)) & jnp.logical_not(meets(d))

    def below(d):
        return (rank(up_z(d)) < rank(z)) & jnp.logical_not(meets(d))

    waits = len(known) - (square0 | row0 | outer0).astype(jnp.int32)
    answers = jnp.int32(0)

    @pl.when(jnp.logical_not(first))
    def _():
        for to in known:
            pl.semaphore_signal(barrier, inc=1, device_id=to, device_id_type=MESH)

    def odd_pair(d):
        return (first & (d > 0)) | (column0 & (up_z(d) == 0))

    for d in steps_z:
        tells = (odd_pair(d) & column0) | (jnp.logical_not(odd_pair(d)) & (above(d) | meets(d)))
        hears = (odd_pair(d) & first) | (jnp.logical_not(odd_pair(d)) & (below(d) | meets(d)))
        waits += hears.astype(jnp.int32)
        answers += (above(d) & jnp.logical_not(odd_pair(d))).astype(jnp.int32)

        @pl.when(tells)
        def _(d=d):
            pl.semaphore_signal(barrier, inc=1, device_id=along_z(d), device_id_type=MESH)

    pl.semaphore_wait(barrier, waits)
    for d in steps_z:

        @pl.when(below(d) & jnp.logical_not(odd_pair(d)))
        def _(d=d):
            pl.semaphore_signal(hello, inc=1, device_id=along_z(d), device_id_type=MESH)

    @pl.when(first)
    def _():
        for to in known + [along_z(d) for d in range(1, FAR + 1)]:
            pl.semaphore_signal(hello0, inc=1, device_id=to, device_id_type=MESH)

    def way(d):
        return (0, d - 1) if d > 0 else (1, -d - 1)

    def wait_z(d):
        wait(packed.at[up_z(-d)], z_recv.at[*way(d)])

    def each(low, high, body):
        def step(t, _):
            body(t)
            return 0

        lax.fori_loop(low, high, step, 0)

    def own_copy(t):
        return pltpu.make_async_copy(f_ref.at[:, columns(x, t, c)], raw.at[t, x, y, c], l_sem.at[t])

    def swap_copies(t):
        mine = raw.at[t, x, y, c]
        return [
            remote(
                f_ref.at[:, columns(other(x, dx), t, other(c, dc))],
                mine, s_send.at[t, k], s_recv.at[t, k], group(dx, 0, dc),
            )
            for k, (dx, dc) in enumerate(square)
        ]

    def y_copies(t, src, dx, dc):
        side, cc = other(x, dx), other(c, dc)
        return [
            remote(
                src, raw.at[t, side, y, cc],
                y_send.at[t, k, side, cc], y_recv.at[t, k, side, cc], group(0, dy, 0),
            )
            for k, dy in enumerate((1, 3))
        ]

    neighbours = [group(0, dy, 0) for dy in (1, 3)]
    mates = [group(dx, 0, dc) for dx, dc in square]

    def start(copies, targets, to_first):
        for copy, to in zip(copies, targets):

            @pl.when(is_first(to) == to_first)
            def _(copy=copy):
                copy.start()

    def swap(t, to_first=False):
        start(y_copies(t, f_ref.at[:, columns(x, t, c)], 0, 0), neighbours, to_first)
        start(swap_copies(t), mates, to_first)
        if not to_first:
            own_copy(t).start()

    def spread(t, from_first=False):
        for k, (dx, dc) in enumerate(square):

            @pl.when(is_first(mates[k]) == from_first)
            def _(k=k, dx=dx, dc=dc):
                part = raw.at[t, other(x, dx), y, other(c, dc)]
                wait(part, s_recv.at[t, k])
                start(y_copies(t, part, dx, dc), neighbours, False)

    def spread_to_first(t):
        for dx, dc in square:
            part = raw.at[t, other(x, dx), y, other(c, dc)]
            start(y_copies(t, part, dx, dc), neighbours, True)

    def hand_copy(t, k, cc, at):
        part = raw.at[t, k, at, cc]
        return remote(part, part, w_send.at[t, k, cc], w_recv.at[t, k, cc], group(0, (1, 3)[k], 0))

    def hand_on(t):
        for dc in range(NC):
            cc = other(c, dc)
            for side in range(NX):
                for k in (side, 1 - side):
                    at = up_y(NY - (1, 3)[k])
                    wait(raw.at[t, side, at, cc], y_recv.at[t, k, side, cc])
                    if side == k:
                        hand_copy(t, k, cc, at).start()

    def complete(t):
        for k in range(2):
            for cc in range(NC):
                wait(raw.at[t, k, up_y(2), cc], w_recv.at[t, k, cc])
        own_copy(t).wait()

    def start_z():
        a_copy.wait()
        for d in reversed(steps_z):
            part = packed.at[z]
            remote(part, part, z_send.at[*way(d)], z_recv.at[*way(d)], along_z(d)).start()


    def rest(t):
        spread(t)

        @pl.when(row0)
        def _():
            spread_to_first(t)

    def second_z():
        for far, ds in ((FAR, range(FAR, 0, -1)), (-FAR, range(1 - FAR, 0))):
            wait_z(far)
            for d in ds:
                part, to = packed.at[up_z(-far)], way(d + far)
                remote(part, part, z_send.at[*to], z_recv.at[*to], along_z(d)).start()

    each(0, 1, swap)

    @pl.when(late & (answers == 0))
    def _():
        start_z()

    each(1, CHUNKS, swap)

    @pl.when(late & (answers > 0))
    def _():
        pl.semaphore_wait(hello, answers)
        start_z()

    spread(0)

    @pl.when(square0 | row0 | outer0 | column0)
    def _():
        pl.semaphore_wait(hello0, 1)
        each(0, CHUNKS, lambda t: swap(t, True))

        @pl.when(row0)
        def _():
            spread_to_first(0)

    @pl.when(late)
    def _():
        second_z()

    def hello_z():
        pl.semaphore_wait(hello, answers)
        start_z()

    @pl.when((z >= FAR) & (z < NZ // 2))
    def _():
        hello_z()

    rest(1)

    @pl.when((z >= FAR) & (z < NZ // 2))
    def _():
        second_z()

    @pl.when(z < FAR)
    def _():
        hello_z()

    each(2, CHUNKS, rest)

    @pl.when(z < FAR)
    def _():
        second_z()

    @pl.when(square0)
    def _():
        each(0, CHUNKS, lambda t: spread(t, True))


    for d in range(1, NZ // 2 + 1):
        for s in (1, -1):
            if d != FAR and s * d != -NZ // 2:
                wait_z(s * d)
    for k in range(NZ // 2):
        anc[xh, x, c, :, k * 128 : k * 128 + 128] = packed[2 * k : 2 * k + 2].reshape(128, ROWS).T

    def rows(h, low, cc, half):
        return anc.at[h, low, cc, half * 64 : half * 64 + 64]

    for first in range(2):
        for k, d in enumerate((1, 3)):
            half = (k + first) % 2
            part = rows(xh, x, c, half)
            send(part, part, x_send.at[k, half], x_recv.at[k, half], along_x(d))
    send(anc.at[xh, x, c], anc.at[xh, x, c], x_send.at[2, 0], x_recv.at[2, 0], core_mate)

    each(0, 2, hand_on)

    for first in range(2):
        for k, d in enumerate((1, 3)):
            half = (k + first) % 2
            part = rows(*chip_x(2 * NX - d), c, half)
            wait(part, x_recv.at[k, half])
            if first == 0:
                send(part, part, x_send.at[3, k], x_recv.at[3, k], along_x(d))
            send(part, part, x_send.at[4 + k, half], x_recv.at[4 + k, half], core_mate)
    each(2, CHUNKS, hand_on)

    def keep(t):
        complete(t)

        def keep_block(g):
            one = jnp.full((ROWS, SEG), pat_ref[0, g].astype(F32), F32).astype(BF16)
            side, yy, cc = g // (NY * NC), lax.rem(g // NC, NY), lax.rem(g, NC)
            masked[t, side, yy, cc] = raw[t, side, yy, cc] * one

        each(0, NX * NY * NC, keep_block)

    def result_copy(t, k):
        dx, dc = square[k]
        part, there = cov.at[t, other(x, dx), other(c, dc)], out_ref.at[:, columns(x, t, c)]
        return remote(part, there, o_send.at[t, k], o_recv.at[t, k], group(dx, 0, dc))

    def own_result(t):
        return pltpu.make_async_copy(cov.at[t, x, c], out_ref.at[:, columns(x, t, c)], o_local.at[t])

    def near_forward():
        for k in range(2):
            part = rows(*chip_x(2), c, k)
            wait(part, x_recv.at[3, k])
            remote(part, part, x_send.at[6, k], x_recv.at[6, k], core_mate).start()

    def near_ready():
        wait(anc.at[xh, x, other(c, 1)], x_recv.at[2, 0])
        for k in range(2):
            wait(rows(*chip_x(2), other(c, 1), k), x_recv.at[6, k])

    def product(i):
        far = (i < 3) | (i == 5)
        t = jnp.where(i < 3, i, jnp.where(i < 5, i - 3, jnp.where(i == 5, 3, i - 4)))
        side = jnp.where(far, 1 - x, x)

        @pl.when(i == 2)
        def _():
            near_forward()

        @pl.when(far)
        def _():
            keep(t)

        @pl.when(i == 3)
        def _():
            near_ready()

        total = jnp.zeros((NC * ROWS, SEG), F32)
        for h in range(2):
            total += jnp.dot(
                anc[h, side].reshape(NC * ROWS, DEEP), masked[t, h].reshape(DEEP, SEG), preferred_element_type=F32
            )
        cross = -total
        terms = masked[t, side, y].reshape(NC * ROWS, SEG).astype(F32) * cross
        vpart[t] += jnp.sum(terms.reshape(NC * ROWS // 8, 8, SEG), axis=0)
        cov[t, side] = cross.astype(BF16).reshape(NC, ROWS, SEG)

        @pl.when(far)
        def _():
            result_copy(t, 1).start()
            result_copy(t, 2).start()

        @pl.when(jnp.logical_not(far))
        def _():
            result_copy(t, 0).start()
            own_result(t).start()

    def far_ready():
        for k, d in enumerate((1, 3)):
            for half in range(2):
                wait(rows(*chip_x(2 * NX - d), other(c, 1), half), x_recv.at[4 + k, half])

    def core_rows(cc):
        total = jnp.zeros((ROWS, SEG), F32)
        for h in range(2):
            total += jnp.dot(anc[h, 1 - x, cc], masked[0, h].reshape(DEEP, SEG), preferred_element_type=F32)
        cross = -total
        terms = masked[0, 1 - x, y, cc].astype(F32) * cross
        vpart[0] += jnp.sum(terms.reshape(ROWS // 8, 8, SEG), axis=0)
        cov[0, 1 - x, cc] = cross.astype(BF16)

        @pl.when(cc == c)
        def _():
            result_copy(0, 1).start()

        @pl.when(cc != c)
        def _():
            result_copy(0, 2).start()

    vpart[...] = jnp.zeros_like(vpart)
    for copy in small:
        copy.wait()
    keep(0)
    core_rows(c)
    far_ready()
    core_rows(1 - c)
    each(1, 2 * CHUNKS, product)

    for k, dy in enumerate((1, 2, 3)):
        send(vpart.at[up_y(dy)], vgot.at[k], v_send.at[k], v_recv.at[k], group(0, dy, 0))

    def results(t):
        for k, (dx, dc) in enumerate(square):
            wait(out_ref.at[:, columns(other(x, dx), t, other(c, dc))], o_recv.at[t, k])
        own_result(t).wait()

    each(0, CHUNKS, results)
    total = vpart[y]
    for k in range(3):
        wait(vgot.at[k], v_recv.at[k])
        total += vgot[k]
    var_ref[...] = piv_ref[...] - jnp.sum(total, axis=0, keepdims=True)
    for handle in sends:
        handle.wait_send()
    for k in range(2):
        remote(rows(xh, x, c, k), rows(xh, x, c, k), x_send.at[6, k], x_recv.at[6, k], core_mate).wait_send()
    for d in range(1 - NZ // 2, NZ // 2 + 1):
        if d:
            remote(packed.at[z], packed.at[z], z_send.at[*way(d)], z_recv.at[*way(d)], core_mate).wait_send()

    def sent(t):
        for copy in swap_copies(t):
            copy.wait_send()
        for dx in range(NX):
            for dc in range(NC):
                for copy in y_copies(t, raw.at[t, x, y, c], dx, dc):
                    copy.wait_send()
        for k in range(2):
            for cc in range(NC):
                hand_copy(t, k, cc, y).wait_send()
        for k in range(3):
            result_copy(t, k).wait_send()

    each(0, CHUNKS, sent)


def hand_over(cross_ref, var_ref, cross_out, var_out, cross, var, sems):
    parts = [pl.ds(k * ROWS // 8, ROWS // 8) for k in range(8)]
    through = [(cross_ref.at[p], cross.at[p], cross_out.at[0, p]) for p in parts] + [(var_ref, var, var_out)]
    loads = [pltpu.make_async_copy(a, b, sems.at[k]) for k, (a, b, _) in enumerate(through)]
    stores = [pltpu.make_async_copy(b, c, sems.at[9 + k]) for k, (_, b, c) in enumerate(through)]
    for load in loads:
        load.start()
    for load, store in zip(loads, stores):
        load.wait()
        store.start()
    for store in stores:
        store.wait()


def on_device(ancestor_inverse, factor_block, block_pattern, pivot_inverse):
    rows, wide = factor_block.shape[1:]
    dma = pltpu.SemaphoreType.DMA
    vmem, hbm = pl.BlockSpec(memory_space=pltpu.VMEM), pl.BlockSpec(memory_space=pltpu.HBM)
    cross_cov, variances = pl.pallas_call(
        kernel,
        out_shape=(
            jax.ShapeDtypeStruct((rows, wide), BF16),
            jax.ShapeDtypeStruct(pivot_inverse.shape, F32),
        ),
        in_specs=[hbm] * 4,
        out_specs=(hbm, vmem),
        scratch_shapes=[
            pltpu.VMEM((CHUNKS, NX, NY, NC, ROWS, SEG), BF16),
            pltpu.VMEM((CHUNKS, NX, NY, NC, ROWS, SEG), BF16),
            pltpu.VMEM((2, NX, NC, ROWS, DEEP), BF16),
            pltpu.VMEM((NZ, 64, ROWS), BF16),
            pltpu.VMEM((CHUNKS, NX, NC, ROWS, SEG), BF16),
            pltpu.VMEM((CHUNKS, 8, SEG), F32),
            pltpu.VMEM((3, 8, SEG), F32),
            pltpu.SMEM(block_pattern.shape, jnp.int32),
            pltpu.VMEM(pivot_inverse.shape, F32),
            pltpu.SemaphoreType.REGULAR, pltpu.SemaphoreType.REGULAR, dma, dma((2,)), dma((CHUNKS, 3)), dma((CHUNKS, 3)), dma((CHUNKS,)),
            dma((CHUNKS, 2, 2, 2)), dma((CHUNKS, 2, 2, 2)), dma((CHUNKS, 2, 2)), dma((CHUNKS, 2, 2)),
            dma((2, 8)), dma((2, 8)), dma((7, 2)), dma((7, 2)),
            dma((CHUNKS, 3)), dma((CHUNKS, 3)), dma((CHUNKS,)), dma((3,)), dma((3,)),
        ],
        compiler_params=pltpu.CompilerParams(
            collective_id=0, has_side_effects=True, vmem_limit_bytes=60 << 20
        ),
    )(ancestor_inverse.T, factor_block[0], block_pattern, pivot_inverse)
    return pl.pallas_call(
        hand_over,
        out_shape=(
            jax.ShapeDtypeStruct((1, rows, wide), BF16),
            jax.ShapeDtypeStruct(pivot_inverse.shape, F32),
        ),
        in_specs=[hbm, hbm],
        out_specs=(hbm, hbm),
        scratch_shapes=[pltpu.VMEM((rows, wide), BF16), pltpu.VMEM(pivot_inverse.shape, F32), dma((18,))],
        compiler_params=pltpu.CompilerParams(vmem_limit_bytes=60 << 20),
    )(cross_cov, variances)


def solution(mesh):
    return jax.shard_map(
        on_device,
        mesh=mesh,
        in_specs=(P("grid", "leaf"), P("leaf", "grid", None), P("leaf", None), P("leaf", "grid")),
        out_specs=(P("leaf", "grid", None), P("leaf", "grid")),
        check_vma=False,
    )
```
